32 devices in a mesh: dom: 4 (over x, core), band: 8 (over z, y).
Axes of the slice: x: 2, y: 2, z: 4, core: 2. Of those that a mesh axis runs over, the one named last changes fastest.
Arguments:
- wavefunctions: bfloat16 [128, 32, 128, 128], P('band', 'dom'), may hold values from -6 to 6
- potential: float32 [32, 128, 128], P('dom'), may hold values from -3 to 1
- projectors: bfloat16 [144, 8, 1024], P('dom'), may hold values from -0.1875 to 0.1875
- margin_atoms: int32 [144], P('dom'), may hold values from 0 to 47, as said below
- tile_rows: int32 [144], P('dom'), may hold values from 0 to 1016
- coupling: float32 [8, 8], replicated, may hold values from -4 to 4
- band_weights: float32 [128], P('band'), may hold values from 0.005 to 0.03
Outputs:
- applied: bfloat16 [128, 32, 128, 128], P('band', 'dom')
- forces: float32 [3, 48], P(None, 'dom')
The draws below stay inside these ranges and needn't reach their ends.
Inputs may be any that keep to these rules, and one draw needn't show every extreme that they name: `margin_atoms`: the list of domain d holds each atom a with a // 12 equal to d - 1, d or d + 1 (cyclically over the domains) exactly once, in an order drawn from the seed; so every atom is listed in three domains.
All inputs are finite; a program needn't handle non-finite values.
Results may differ from the reference program's by a relative error of at most 0.0095.
Values may be sent and summed in bfloat16 or wider, within the bound.
A program may use at most 128 MiB of HBM per device.

```python
import jax
import jax.numpy as jnp
from jax import lax

NB = 128
NPROJ = 8
CX = 8
NY = 128
NZ = 128
TROWS = 8
ATOM_DEV = 12
ENT_DEV = 36
NX = 32
ATOMS = 48
ENTRIES = 144
N_DOM = 4


def draw_margin_atoms(key, part):
    key = jax.random.fold_in(key, 5)
    atom_count = ATOM_DEV * N_DOM
    domain = jnp.arange(N_DOM, dtype=jnp.int32)[:, None]
    position = jnp.arange(3 * ATOM_DEV, dtype=jnp.int32)[None, :]
    source = ((domain - 1) * ATOM_DEV + position + atom_count) % atom_count
    keys = jax.random.split(key, N_DOM)
    orders = jax.vmap(lambda one_key: jax.random.permutation(one_key, 3 * ATOM_DEV))(keys).astype(jnp.int32)
    return jnp.take_along_axis(source, orders, 1).reshape(-1).astype(jnp.int32)


def place_ends(drawn, key, low, high):
    index_at = [jax.random.randint(jax.random.fold_in(key, axis), (), 0, length) for axis, length in enumerate(drawn.shape)]
    main_axis = drawn.shape.index(max(drawn.shape))
    neighbour = index_at[:main_axis] + [(index_at[main_axis] + 1) % drawn.shape[main_axis]] + index_at[main_axis + 1:]
    return drawn.at[tuple(index_at)].set(low).at[tuple(neighbour)].set(high)


def level_of(key, shape, cuts, least, high):
    level, own = 1.0, jax.random.fold_in(key, 6)
    for dim, parts in cuts:
        heights = jnp.exp(jax.random.uniform(jax.random.fold_in(own, dim), (parts,), jnp.float32, least / len(cuts), high / len(cuts)))
        level = level * jnp.repeat(heights, shape[dim] // parts).reshape([-1 if axis == dim else 1 for axis in range(len(shape))])
    return level


def noise(own_key, shape, spread, bound, pieces=(), held_as=jnp.bfloat16):
    loudness = level_of(own_key, shape, pieces, -0.22, 0.18) if pieces else 1.0
    entries = jax.random.normal(own_key, shape, jnp.float32) * spread * loudness
    return jnp.minimum(jnp.maximum(entries, -bound), bound).astype(held_as)


def setup_inputs(seed: int = 0) -> dict:
    key_of = jax.random.split(jax.random.key(seed), 8)
    wavefunctions = noise(key_of[0], (NB, NX, NY, NZ), 1.0, 6.0, ((0, 8), (1, 4)))
    potential = jnp.clip(-3.0 + 4.0 * jax.random.uniform(key_of[1], (NX, NY, NZ), jnp.float32) ** level_of(key_of[1], (NX, NY, NZ), ((0, 4),), -0.2, 0.2), -3.0, 1.0)
    projectors = noise(key_of[2], (ENTRIES, NPROJ, TROWS * NZ), (TROWS * NZ) ** -0.5, 0.1875, ((0, 4),))
    margin_atoms = draw_margin_atoms(jax.random.fold_in(key_of[7], 71), 0)
    tile_rows = place_ends(jax.random.randint(key_of[4], (ENTRIES,), 0, CX * NY - TROWS + 1), jax.random.fold_in(key_of[4], 1), 0, CX * NY - TROWS).astype(jnp.int32)
    coupling = noise(key_of[5], (NPROJ, NPROJ), 1.0, 4.0, (), jnp.float32)
    band_weights = jnp.clip(0.005 + 0.024999999 * jax.random.uniform(key_of[6], (NB,), jnp.float32) ** level_of(key_of[6], (NB,), ((0, 8),), -0.2, 0.2), 0.005, 0.03)
    return {"wavefunctions": wavefunctions, "potential": potential, "projectors": projectors, "margin_atoms": margin_atoms, "tile_rows": tile_rows, "coupling": coupling, "band_weights": band_weights}


second_coef = (-1.0 / 12.0, 4.0 / 3.0, -2.5, 4.0 / 3.0, -1.0 / 12.0)
first_coef = (1.0 / 12.0, -2.0 / 3.0, 0.0, 2.0 / 3.0, -1.0 / 12.0)


def derivative(real_band, along_axis, stencil):
    summed = jnp.zeros_like(real_band)
    for offset in range(-2, 3):
        if stencil[offset + 2] != 0.0:
            summed = summed + stencil[offset + 2] * jnp.roll(real_band, -offset, along_axis)
    return summed


def tile_index(tile_rows):
    entry_count = tile_rows.shape[0]
    domain = jnp.arange(entry_count, dtype=jnp.int32) // ENT_DEV
    first_row = domain * (CX * NY) + tile_rows
    return (first_row[:, None] + jnp.arange(TROWS, dtype=jnp.int32)[None, :]).reshape(-1)


def reference(wavefunctions, potential, projectors, margin_atoms, tile_rows, coupling, band_weights):
    gather_rows = tile_index(tile_rows)
    entry_count = tile_rows.shape[0]
    proj_real = projectors.astype(jnp.float32)

    def measure_band(one_band):
        real_band = one_band.astype(jnp.float32)
        gradients = [derivative(real_band, along_axis, first_coef).astype(jnp.bfloat16) for along_axis in range(3)]
        stacked = jnp.stack([one_band] + gradients)
        tile_values = stacked.reshape(4, NX * NY, NZ)[:, gather_rows].reshape(4, entry_count, TROWS * NZ)
        return jnp.einsum('qet,eit->eqi', tile_values.astype(jnp.float32), proj_real)

    measured = lax.map(measure_band, wavefunctions)
    atom_table = jax.ops.segment_sum(measured.transpose(1, 2, 0, 3), margin_atoms, num_segments=ATOMS)
    margins = atom_table[:, 0]
    force_margins = atom_table[:, 1:4]
    symmetric = 0.5 * (coupling + coupling.T)
    scaled = jnp.einsum('abj,ij->abi', margins, symmetric, precision=lax.Precision.HIGHEST)
    forces = -2.0 * jnp.einsum('abi,akbi,b->ka', scaled, force_margins, band_weights, precision=lax.Precision.HIGHEST)
    scaled_half = scaled.astype(jnp.bfloat16)
    entry_coef = scaled_half[margin_atoms].astype(jnp.float32).transpose(1, 0, 2)

    def apply_band(inputs):
        one_band, coef_band = inputs
        real_band = one_band.astype(jnp.float32)
        laplace_term = derivative(real_band, 0, second_coef) + derivative(real_band, 1, second_coef) + derivative(real_band, 2, second_coef)
        local_part = -0.5 * laplace_term + potential * real_band
        tile_terms = jnp.einsum('ei,eit->et', coef_band, proj_real).reshape(entry_count * TROWS, NZ)
        nonlocal_part = jnp.zeros((NX * NY, NZ), jnp.float32).at[gather_rows].add(tile_terms)
        return (local_part + nonlocal_part.reshape(NX, NY, NZ)).astype(jnp.bfloat16)

    applied = lax.map(apply_band, (wavefunctions, entry_coef))
    return applied, forces
```

```python
import functools

import jax
import jax.numpy as jnp
import numpy as np
from jax import lax
from jax.experimental import pallas as pl
from jax.experimental.pallas import tpu as pltpu
from jax.sharding import PartitionSpec as P

ATOM_DEV = 12
LANES = 128
ROWS = 16
VMEM_LIMIT = 52 * 1024 * 1024
F32 = jnp.float32
BF16 = jnp.bfloat16
HIGHEST = lax.Precision.HIGHEST


def vmem():
    return pl.BlockSpec(memory_space=pltpu.VMEM)


def smem():
    return pl.BlockSpec(memory_space=pltpu.SMEM)


def dot(a, b):
    return jnp.dot(a, b, preferred_element_type=F32)


def dot_nt(a, b, precision=None):
    return lax.dot_general(
        a, b, (((1,), (1,)), ((), ())), precision=precision, preferred_element_type=F32
    )


def circulant(width, taps):
    table = np.zeros((width, width), np.float32)
    for offset, value in taps.items():
        for target in range(width):
            table[(target + offset) % width, target] += value
    return table


def band_swap(band_count, band_pad):
    table = np.zeros((ROWS * band_pad, band_count * ROWS), np.float32)
    for y in range(ROWS):
        for b in range(band_count):
            table[y * band_pad + b, b * ROWS + y] = 1.0
    return table


def measure_tiles(field_ref, proj_ref, rows_ref, lhs_ref, meas_ref, entry_count, proj_count, depth):
    height = field_ref.shape[1]
    group = LANES // proj_count
    meas_ref[...] = jnp.zeros_like(meas_ref)
    for start in range(0, entry_count, group):
        count = min(group, entry_count - start)
        for k in range(count):
            row = rows_ref[start + k]
            tile = field_ref[pl.ds(row, depth)]
            for j in range(depth):
                lhs_ref[k * height : (k + 1) * height, j * LANES : (j + 1) * LANES] = tile[j]
        width = count * proj_count
        whole = dot_nt(
            lhs_ref[: count * height],
            proj_ref[start * proj_count : start * proj_count + width],
        )
        whole = whole.reshape(count, height, width)
        lane = lax.broadcasted_iota(jnp.int32, (count, height, width), 2) // proj_count
        item = lax.broadcasted_iota(jnp.int32, (count, height, width), 0)
        picked = jnp.sum(jnp.where(lane == item, whole, 0.0), axis=0)
        meas_ref[:, start * proj_count : start * proj_count + width] = picked


def margin_kernel(
    dims, wave_ref, proj_ref, rows_ref, swap_ref, sort_ref, turned_ref, table_ref, lhs_ref, meas_ref
):
    band_count, band_pad, plane_count, width_y, entry_count, proj_count, depth = dims

    def turn(step, carry):
        for x in range(plane_count):
            block = wave_ref[:, x, pl.ds(pl.multiple_of(step * ROWS, ROWS), ROWS), :]
            moved = dot(swap_ref[...], block.reshape(band_count * ROWS, LANES)).astype(BF16)
            turned_ref[pl.ds(x * width_y + step * ROWS, ROWS)] = moved.reshape(
                ROWS, band_pad, LANES
            )
        return carry

    lax.fori_loop(0, width_y // ROWS, turn, 0)
    measure_tiles(
        turned_ref, proj_ref, rows_ref, lhs_ref, meas_ref, entry_count, proj_count, depth
    )
    table_ref[...] = dot(meas_ref[...].astype(BF16), sort_ref[...]).astype(BF16)


def gradient_kernel(
    dims, turned_ref, proj_ref, rows_ref, first_ref, meas_ref, field_ref, lhs_ref
):
    band_count, band_pad, plane_count, width_y, entry_count, proj_count, depth = dims

    def rows_of(x, y, count):
        return turned_ref[pl.ds(x * width_y + y, count)].astype(F32)

    def step_rows(step, carry):
        y = step * ROWS
        before = lax.rem(y + width_y - 2, width_y)
        after = lax.rem(y + ROWS, width_y)
        for x in range(plane_count):
            here = turned_ref[pl.ds(x * width_y + y, ROWS)]
            wide = jnp.concatenate(
                [rows_of(x, before, 2), here.astype(F32), rows_of(x, after, 2)], axis=0
            )
            along_y = wide[:ROWS] - wide[4:] + 8.0 * (wide[3 : ROWS + 3] - wide[1 : ROWS + 1])
            along_x = jnp.zeros((ROWS, band_pad, LANES), F32)
            for offset, value in ((-2, 1.0), (-1, -8.0), (1, 8.0), (2, -1.0)):
                if 0 <= x + offset < plane_count:
                    along_x = along_x + value * rows_of(x + offset, y, ROWS)
            along_z = dot(here.reshape(ROWS * band_pad, LANES), first_ref[...]).reshape(
                ROWS, band_pad, LANES
            )
            rows = pl.ds(x * width_y + y, ROWS)
            field_ref[rows, :band_pad] = (along_x * (1.0 / 12.0)).astype(BF16)
            field_ref[rows, band_pad : 2 * band_pad] = (along_y * (1.0 / 12.0)).astype(BF16)
            field_ref[rows, 2 * band_pad :] = (along_z * (1.0 / 12.0)).astype(BF16)
        return carry

    lax.fori_loop(0, width_y // ROWS, step_rows, 0)
    measure_tiles(field_ref, proj_ref, rows_ref, lhs_ref, meas_ref, entry_count, proj_count, depth)


def apply_kernel(
    dims, places, *refs
):
    band_count, band_pad, plane_count, width_y, entry_count, proj_count, depth = dims
    table_refs = refs[: len(places)]
    (
        wave_ref, pot_ref, proj_ref, rows_ref, swap_ref, sort_ref, mix_ref, second_y_ref,
        second_z_ref, out_ref, edge_ref, coef_ref, acc_ref, part_ref,
    ) = refs[len(places) :]
    shifts = dict(places)
    scaled = []
    for s in (-1, 0, 1):
        total = jnp.zeros((band_pad, LANES), F32)
        for u in (s - 1, s, s + 1):
            block = s - u + 1
            held = table_refs[shifts[u]][:, block * LANES : (block + 1) * LANES]
            total = total + held.astype(F32)
        scaled.append(jnp.dot(total, mix_ref[...], precision=HIGHEST, preferred_element_type=F32))
    scaled = jnp.concatenate(scaled, axis=1)
    coef = dot_nt(scaled, sort_ref[...].astype(F32), HIGHEST)
    coef_ref[...] = coef
    half = coef.astype(BF16)

    acc_ref[...] = jnp.zeros_like(acc_ref)
    group = LANES // proj_count
    for start in range(0, entry_count, group):
        count = min(group, entry_count - start)
        width = count * proj_count
        first = start * proj_count
        held = jnp.broadcast_to(
            half[:, first : first + width].astype(F32)[None], (count, band_pad, width)
        )
        lane = lax.broadcasted_iota(jnp.int32, (count, band_pad, width), 2) // proj_count
        item = lax.broadcasted_iota(jnp.int32, (count, band_pad, width), 0)
        spread = jnp.where(lane == item, held, 0.0).reshape(count * band_pad, width).astype(BF16)
        for j in range(depth):
            terms = dot(
                spread, proj_ref[first : first + width, j * LANES : (j + 1) * LANES]
            )
            for k in range(count):
                row = rows_ref[start + k] + j
                acc_ref[row] += terms[k * band_pad : (k + 1) * band_pad]

    def turn_back(step, carry):
        for x in range(plane_count):
            block = acc_ref[pl.ds(x * width_y + step * ROWS, ROWS)].astype(BF16)
            moved = lax.dot_general(
                swap_ref[...],
                block.reshape(ROWS * band_pad, LANES),
                (((0,), (0,)), ((), ())),
                preferred_element_type=F32,
            ).astype(BF16)
            part_ref[:, x, pl.ds(pl.multiple_of(step * ROWS, ROWS), ROWS), :] = moved.reshape(
                band_count, ROWS, LANES
            )
        return carry

    lax.fori_loop(0, width_y // ROWS, turn_back, 0)

    def each_band(b, carry):
        for x in range(plane_count):
            here = wave_ref[b, x]
            lap = dot(second_y_ref[...], here) + dot(here, second_z_ref[...])
            for offset, value in ((-2, -1.0), (-1, 16.0), (1, 16.0), (2, -1.0)):
                if 0 <= x + offset < plane_count:
                    lap = lap + value * wave_ref[b, x + offset].astype(F32)
            total = lap * (-1.0 / 24.0) + pot_ref[x] * here.astype(F32)
            total = total + part_ref[b, x].astype(F32)
            if x < 2:
                edge_ref[b, x] = total
            elif x >= plane_count - 2:
                edge_ref[b, x - plane_count + 4] = total
            else:
                out_ref[b, x] = total.astype(BF16)
        return carry

    lax.fori_loop(0, band_count, each_band, 0)


def force_kernel(
    dims, before_ref, after_ref, proj_ref, rows_ref, swap_ref, meas_ref, coef_ref, weight_ref,
    pick_ref, out_ref, field_ref, lhs_ref, extra_ref,
):
    band_count, band_pad, plane_count, width_y, entry_count, proj_count, depth = dims
    inner = (plane_count - 4) * width_y
    field_ref[2 * width_y : 2 * width_y + inner] = jnp.zeros((inner, band_pad, LANES), BF16)

    def step_rows(step, carry):
        rows = pl.ds(pl.multiple_of(step * ROWS, ROWS), ROWS)
        b2 = before_ref[:, 0, rows, :].astype(F32)
        b1 = before_ref[:, 1, rows, :].astype(F32)
        a1 = after_ref[:, 0, rows, :].astype(F32)
        a2 = after_ref[:, 1, rows, :].astype(F32)
        last = plane_count - 1
        for x, value in ((0, b2 - 8.0 * b1), (1, b1), (last - 1, -a1), (last, 8.0 * a1 - a2)):
            value = (value * (1.0 / 12.0)).astype(BF16)
            moved = dot(swap_ref[...], value.reshape(band_count * ROWS, LANES)).astype(BF16)
            field_ref[pl.ds(x * width_y + step * ROWS, ROWS)] = moved.reshape(
                ROWS, band_pad, LANES
            )
        return carry

    lax.fori_loop(0, width_y // ROWS, step_rows, 0)
    measure_tiles(
        field_ref, proj_ref, rows_ref, lhs_ref, extra_ref, entry_count, proj_count, depth
    )
    weighted = coef_ref[...] * weight_ref[...]
    sums = []
    for k in range(3):
        held = meas_ref[k * band_pad : (k + 1) * band_pad]
        if k == 0:
            held = held + extra_ref[...]
        sums.append(jnp.sum(weighted * held, axis=0, keepdims=True))
    sums = jnp.concatenate(sums + [jnp.zeros((5, sums[0].shape[1]), F32)], axis=0)
    for s in range(3):
        out_ref[s] = jnp.dot(
            sums,
            pick_ref[:, s * LANES : (s + 1) * LANES].astype(F32),
            precision=HIGHEST,
            preferred_element_type=F32,
        )


def reduce_kernel(dom_count, band_devices, part_ref, out_ref, held_ref, send_sem, recv_sem):
    own = lax.axis_index("dom")
    band = lax.axis_index("band")
    partners = [
        (s, t) for t in range(band_devices) for s in (-1, 0, 1) if (s, t) != (0, 0)
    ]

    def device(s, t):
        return {
            "dom": lax.rem(own + s + dom_count, dom_count),
            "band": lax.rem(band + t, band_devices),
        }

    barrier = pltpu.get_barrier_semaphore()
    for s, t in partners:
        pl.semaphore_signal(
            barrier, inc=1, device_id=device(s, t), device_id_type=pl.DeviceIdType.MESH
        )
    pl.semaphore_wait(barrier, len(partners))
    copies = []
    for s, t in partners:
        slot = (s + 1) * band_devices + t
        copy = pltpu.make_async_remote_copy(
            src_ref=part_ref.at[s + 1],
            dst_ref=held_ref.at[slot],
            send_sem=send_sem.at[slot],
            recv_sem=recv_sem.at[slot],
            device_id=device(s, t),
            device_id_type=pl.DeviceIdType.MESH,
        )
        copy.start()
        copies.append((slot, copy))
    total = part_ref[1]
    for slot, copy in copies:
        copy.wait_recv()
        total = total + held_ref[slot]
    for slot, copy in copies:
        copy.wait_send()
    out_ref[...] = total


def edge_kernel(edge_ref, before_ref, after_ref, inner_ref, out_ref):
    side = pl.program_id(1)

    @pl.when(side == 0)
    def _():
        b2 = before_ref[:, 0].astype(F32)
        b1 = before_ref[:, 1].astype(F32)
        out_ref[:, 0] = (edge_ref[:, 0] + (b2 - 16.0 * b1) * (1.0 / 24.0)).astype(BF16)
        out_ref[:, 1] = (edge_ref[:, 1] + b1 * (1.0 / 24.0)).astype(BF16)

    @pl.when(side == 1)
    def _():
        a1 = after_ref[:, 0].astype(F32)
        a2 = after_ref[:, 1].astype(F32)
        out_ref[:, 0] = (edge_ref[:, 0] + a1 * (1.0 / 24.0)).astype(BF16)
        out_ref[:, 1] = (edge_ref[:, 1] + (a2 - 16.0 * a1) * (1.0 / 24.0)).astype(BF16)


def per_device(
    wavefunctions, potential, projectors, margin_atoms, tile_rows, coupling, band_weights
):
    band_count, plane_count, width_y, width_z = wavefunctions.shape
    entry_count, proj_count, tile_len = projectors.shape
    depth = tile_len // width_z
    row_count = plane_count * width_y
    band_pad = max(band_count, ROWS)
    dims = (band_count, band_pad, plane_count, width_y, entry_count, proj_count, depth)
    dom_count = lax.axis_size("dom")
    band_devices = lax.axis_size("band")
    own_index = lax.axis_index("dom")

    up = [(i, (i + 1) % dom_count) for i in range(dom_count)]
    down = [(j, i) for i, j in up]
    before = lax.ppermute(wavefunctions[:, plane_count - 2 :], "dom", up)
    after = lax.ppermute(wavefunctions[:, :2], "dom", down)

    params = pltpu.CompilerParams(vmem_limit_bytes=VMEM_LIMIT)
    swap = jnp.asarray(band_swap(band_count, band_pad), BF16)
    first_z = jnp.asarray(circulant(width_z, {-2: 1.0, -1: -8.0, 1: 8.0, 2: -1.0}), BF16)
    second_z = jnp.asarray(
        circulant(width_z, {-2: -1.0, -1: 16.0, 0: -90.0, 1: 16.0, 2: -1.0}), BF16
    )
    second_y = jnp.asarray(circulant(width_y, {-2: -1.0, -1: 16.0, 1: 16.0, 2: -1.0}), BF16)

    relative = lax.rem(margin_atoms // ATOM_DEV - own_index + 1 + dom_count, dom_count)
    entry_lanes = -(-entry_count * proj_count // LANES) * LANES
    lane = jnp.arange(entry_lanes, dtype=jnp.int32)
    spare = (0, entry_lanes // proj_count - entry_count)
    first_lane = jnp.pad(
        relative * LANES + (margin_atoms % ATOM_DEV) * proj_count, spare, constant_values=-LANES
    )
    pick_lane = jnp.pad(
        relative * LANES + margin_atoms % ATOM_DEV, spare, constant_values=-LANES
    )
    target = jnp.arange(3 * LANES, dtype=jnp.int32)[None, :]
    first_lane = jnp.repeat(first_lane, proj_count) + lane % proj_count
    sort = (first_lane[:, None] == target).astype(BF16)
    pick = (jnp.repeat(pick_lane, proj_count)[:, None] == target).astype(BF16)
    symmetric = 0.5 * (coupling + coupling.T)
    mix = jnp.kron(jnp.eye(LANES // proj_count, dtype=F32), symmetric)
    weights = jnp.pad(-2.0 * band_weights, (0, band_pad - band_count))[:, None]
    flat = projectors.reshape(entry_count * proj_count, tile_len)
    group = LANES // proj_count

    turned, table = pl.pallas_call(
        functools.partial(margin_kernel, dims),
        out_shape=(
            jax.ShapeDtypeStruct((row_count, band_pad, width_z), BF16),
            jax.ShapeDtypeStruct((band_pad, 3 * LANES), BF16),
        ),
        in_specs=[vmem(), vmem(), smem(), vmem(), vmem()],
        out_specs=(vmem(), vmem()),
        scratch_shapes=[
            pltpu.VMEM((group * band_pad, tile_len), BF16),
            pltpu.VMEM((band_pad, entry_lanes), F32),
        ],
        compiler_params=params,
        cost_estimate=pl.CostEstimate(flops=1 << 31, bytes_accessed=9 << 20, transcendentals=0),
        name="margins",
    )(wavefunctions, flat, tile_rows, swap, sort)

    distinct, places, tables = {}, [], []
    for u in range(-2, 3):
        key = u % dom_count
        if key not in distinct:
            distinct[key] = len(tables)
            if key == 0:
                tables.append(table)
            else:
                pairs = [((i + u) % dom_count, i) for i in range(dom_count)]
                tables.append(lax.ppermute(table, "dom", pairs))
        places.append((u, distinct[key]))

    measured = pl.pallas_call(
        functools.partial(gradient_kernel, dims),
        out_shape=jax.ShapeDtypeStruct((3 * band_pad, entry_lanes), F32),
        in_specs=[vmem(), vmem(), smem(), vmem()],
        out_specs=vmem(),
        scratch_shapes=[
            pltpu.VMEM((row_count, 3 * band_pad, width_z), BF16),
            pltpu.VMEM((3 * group * band_pad, tile_len), BF16),
        ],
        compiler_params=params,
        cost_estimate=pl.CostEstimate(flops=1 << 32, bytes_accessed=9 << 20, transcendentals=0),
        name="gradients",
    )(turned, flat, tile_rows, first_z)

    inner, edge, coef = pl.pallas_call(
        functools.partial(apply_kernel, dims, tuple(places_of(places, tables))),
        out_shape=(
            jax.ShapeDtypeStruct(wavefunctions.shape, BF16),
            jax.ShapeDtypeStruct((band_count, 4, width_y, width_z), F32),
            jax.ShapeDtypeStruct((band_pad, entry_lanes), F32),
        ),
        in_specs=[vmem()] * len(places) + [vmem(), vmem(), vmem(), smem()] + [vmem()] * 5,
        out_specs=(vmem(), vmem(), vmem()),
        scratch_shapes=[
            pltpu.VMEM((row_count, band_pad, width_z), F32),
            pltpu.VMEM(wavefunctions.shape, BF16),
        ],
        compiler_params=params,
        cost_estimate=pl.CostEstimate(flops=1 << 32, bytes_accessed=16 << 20, transcendentals=0),
        name="apply",
    )(
        *[tables[index] for _, index in places], wavefunctions, potential, flat, tile_rows, swap,
        sort, mix, second_y, second_z,
    )

    partial = pl.pallas_call(
        functools.partial(force_kernel, dims),
        out_shape=jax.ShapeDtypeStruct((3, 8, LANES), F32),
        in_specs=[vmem(), vmem(), vmem(), smem()] + [vmem()] * 5,
        out_specs=vmem(),
        scratch_shapes=[
            pltpu.VMEM((row_count, band_pad, width_z), BF16),
            pltpu.VMEM((group * band_pad, tile_len), BF16),
            pltpu.VMEM((band_pad, entry_lanes), F32),
        ],
        compiler_params=params,
        cost_estimate=pl.CostEstimate(flops=1 << 30, bytes_accessed=4 << 20, transcendentals=0),
        name="force_part",
    )(before, after, flat, tile_rows, swap, measured, coef, weights, pick)

    slots = 3 * band_devices
    forces = pl.pallas_call(
        functools.partial(reduce_kernel, dom_count, band_devices),
        out_shape=jax.ShapeDtypeStruct((8, LANES), F32),
        in_specs=[vmem()],
        out_specs=vmem(),
        scratch_shapes=[
            pltpu.VMEM((slots, 8, LANES), F32),
            pltpu.SemaphoreType.DMA((slots,)),
            pltpu.SemaphoreType.DMA((slots,)),
        ],
        compiler_params=pltpu.CompilerParams(collective_id=0, has_side_effects=True),
        name="force_sum",
    )(partial)[:3, :ATOM_DEV]

    chunk = max(band_count // 4, 1)
    applied = pl.pallas_call(
        edge_kernel,
        grid=(band_count // chunk, 2),
        out_shape=jax.ShapeDtypeStruct(wavefunctions.shape, BF16),
        in_specs=[
            pl.BlockSpec((chunk, 2, width_y, width_z), lambda i, side: (i, side, 0, 0)),
            pl.BlockSpec((chunk, 2, width_y, width_z), lambda i, side: (i, 0, 0, 0)),
            pl.BlockSpec((chunk, 2, width_y, width_z), lambda i, side: (i, 0, 0, 0)),
            pl.BlockSpec(memory_space=pl.ANY),
        ],
        out_specs=pl.BlockSpec(
            (chunk, 2, width_y, width_z),
            lambda i, side: (i, side * (plane_count // 2 - 1), 0, 0),
        ),
        input_output_aliases={3: 0},
        compiler_params=params,
        cost_estimate=pl.CostEstimate(flops=1 << 24, bytes_accessed=8 << 20, transcendentals=0),
        name="edges",
    )(edge, before, after, inner)
    return (applied, forces)


def places_of(places, tables):
    return [(u, position) for position, (u, _) in enumerate(places)]


def solution(mesh):
    placed = (
        P("band", "dom", None, None),
        P("dom", None, None),
        P("dom", None, None),
        P("dom"),
        P("dom"),
        P(),
        P("band"),
    )
    return jax.shard_map(
        per_device,
        mesh=mesh,
        in_specs=placed,
        out_specs=(P("band", "dom", None, None), P(None, "dom")),
        check_vma=False,
    )
```

```python
import functools

import jax
import jax.numpy as jnp
import numpy as np
from jax import lax
from jax.experimental import pallas as pl
from jax.experimental.pallas import tpu as pltpu
from jax.sharding import PartitionSpec as P

ATOM_DEV = 12
LANES = 128
ROWS = 16
VMEM_LIMIT = 52 * 1024 * 1024
F32 = jnp.float32
BF16 = jnp.bfloat16
HIGHEST = lax.Precision.HIGHEST
SMALL = pl.CostEstimate(flops=1 << 20, bytes_accessed=1 << 12, transcendentals=0)


def vmem():
    return pl.BlockSpec(memory_space=pltpu.VMEM)


def smem():
    return pl.BlockSpec(memory_space=pltpu.SMEM)


def dot(a, b):
    return jnp.dot(a, b, preferred_element_type=F32)


def dot_nt(a, b, precision=None):
    return lax.dot_general(
        a, b, (((1,), (1,)), ((), ())), precision=precision, preferred_element_type=F32
    )


def circulant(width, taps):
    table = np.zeros((width, width), np.float32)
    for offset, value in taps.items():
        for target in range(width):
            table[(target + offset) % width, target] += value
    return table


def band_swap(band_count, band_pad):
    table = np.zeros((ROWS * band_pad, band_count * ROWS), np.float32)
    for y in range(ROWS):
        for b in range(band_count):
            table[y * band_pad + b, b * ROWS + y] = 1.0
    return table


def pick_groups(whole, count, height, proj_count):
    width = count * proj_count
    whole = whole.reshape(count, height, width)
    lane = lax.broadcasted_iota(jnp.int32, (count, height, width), 2) // proj_count
    item = lax.broadcasted_iota(jnp.int32, (count, height, width), 0)
    return jnp.sum(jnp.where(lane == item, whole, 0.0), axis=0)


def turn_pair(swap, left, right):
    return dot(swap, jnp.concatenate([left, right], axis=1)).astype(BF16)


def signal_all(devices):
    barrier = pltpu.get_barrier_semaphore()
    for device in devices:
        pl.semaphore_signal(
            barrier, inc=1, device_id=device, device_id_type=pl.DeviceIdType.MESH
        )


def wait_all(devices):
    pl.semaphore_wait(pltpu.get_barrier_semaphore(), len(devices))


def margin_kernel(
    dims, dom_count, wave_ref, proj_ref, rows_ref, swap_ref, sort_ref, first_ref, tables_ref,
    meas_ref, turned_ref, proj_z_ref, lhs_ref, both_ref, own_ref, held_ref, send_sem, recv_sem,
):
    band_count, band_pad, plane_count, width_y, entry_count, proj_count, depth = dims
    stride = width_y + 4
    group = LANES // proj_count
    own = lax.axis_index("dom")
    moves = other_moves(dom_count)
    signal_all([{"dom": lax.rem(own + u, dom_count)} for u in moves])

    turned_ref[: 2 * stride] = jnp.zeros((2 * stride, band_pad, LANES), BF16)
    turned_ref[(plane_count + 2) * stride :] = jnp.zeros((2 * stride, band_pad, LANES), BF16)

    def turn(step, carry):
        rows = pl.ds(pl.multiple_of(step * ROWS, ROWS), ROWS)
        for x in range(0, plane_count, 2):
            moved = turn_pair(
                swap_ref[...],
                wave_ref[:, x, rows, :].reshape(band_count * ROWS, LANES),
                wave_ref[:, x + 1, rows, :].reshape(band_count * ROWS, LANES),
            )
            for k in range(2):
                turned_ref[pl.ds((x + k + 2) * stride + 2 + step * ROWS, ROWS)] = moved[
                    :, k * LANES : (k + 1) * LANES
                ].reshape(ROWS, band_pad, LANES)
        return carry

    lax.fori_loop(0, width_y // ROWS, turn, 0)
    for x in range(2, plane_count + 2):
        base = x * stride
        turned_ref[base : base + 2] = turned_ref[base + width_y : base + width_y + 2]
        turned_ref[base + width_y + 2 : base + width_y + 4] = turned_ref[base + 2 : base + 4]

    for j in range(depth):
        columns = slice(j * LANES, (j + 1) * LANES)
        proj_z_ref[:, columns] = (
            dot(proj_ref[:, columns], first_ref[...]) * (-1.0 / 12.0)
        ).astype(BF16)

    def place(row, j):
        at = row + j
        return at + 4 * lax.div(at, width_y) + 2 * stride + 2

    meas_ref[...] = jnp.zeros_like(meas_ref)
    both_ref[...] = jnp.zeros_like(both_ref)
    for start in range(0, entry_count, group):
        count = min(group, entry_count - start)
        width = count * proj_count
        first = start * proj_count

        def fetch(k, carry):
            row = rows_ref[start + k]
            for j in range(depth):
                lhs_ref[k, :band_pad, j * LANES : (j + 1) * LANES] = turned_ref[place(row, j)]
            return carry

        lax.fori_loop(0, count, fetch, 0)
        lhs = lhs_ref[:count, :band_pad].reshape(count * band_pad, depth * LANES)
        whole = dot_nt(lhs, proj_ref[first : first + width])
        both_ref[:, first : first + width] = pick_groups(whole, count, band_pad, proj_count)
        whole = dot_nt(lhs, proj_z_ref[first : first + width])
        meas_ref[2 * band_pad :, first : first + width] = pick_groups(
            whole, count, band_pad, proj_count
        )

    own_ref[...] = dot(both_ref[...].astype(BF16), sort_ref[...]).astype(BF16)
    wait_all(moves)
    copies = []
    for slot, u in enumerate(moves):
        copy = pltpu.make_async_remote_copy(
            src_ref=own_ref,
            dst_ref=held_ref.at[slot],
            send_sem=send_sem.at[slot],
            recv_sem=recv_sem.at[slot],
            device_id={"dom": lax.rem(own + dom_count - u, dom_count)},
            device_id_type=pl.DeviceIdType.MESH,
        )
        copy.start()
        copies.append(copy)

    for start in range(0, entry_count, group):
        count = min(group, entry_count - start)
        width = count * proj_count
        first = start * proj_count

        def derive(k, carry):
            row = rows_ref[start + k]
            for j in range(depth):
                at = place(row, j)
                columns = slice(j * LANES, (j + 1) * LANES)
                for part, step in ((0, stride), (1, 1)):
                    far = turned_ref[at - 2 * step].astype(F32) - turned_ref[
                        at + 2 * step
                    ].astype(F32)
                    near = turned_ref[at + step].astype(F32) - turned_ref[at - step].astype(F32)
                    lhs_ref[k, part * band_pad : (part + 1) * band_pad, columns] = (
                        far * (1.0 / 12.0) + near * (2.0 / 3.0)
                    ).astype(BF16)
            return carry

        lax.fori_loop(0, count, derive, 0)
        lhs = lhs_ref[:count].reshape(count * 2 * band_pad, depth * LANES)
        whole = dot_nt(lhs, proj_ref[first : first + width])
        meas_ref[: 2 * band_pad, first : first + width] = pick_groups(
            whole, count, 2 * band_pad, proj_count
        )

    tables_ref[0] = own_ref[...]
    for slot, copy in enumerate(copies):
        copy.wait_recv()
        tables_ref[slot + 1] = held_ref[slot]
    for copy in copies:
        copy.wait_send()


def apply_kernel(
    dims, places, tables_ref, wave_ref, pot_ref, proj_ref, rows_ref, back_ref, sort_ref, mix_ref,
    second_y_ref, second_z_ref, out_ref, edge_ref, coef_ref, acc_ref, part_ref, scale_ref,
    inner_buf, edge_buf, inner_sem, edge_sem,
):
    band_count, band_pad, plane_count, width_y, entry_count, proj_count, depth = dims
    totals = []
    for s in (-1, 0, 1):
        total = jnp.zeros((band_pad, LANES), F32)
        for u in (s - 1, s, s + 1):
            block = s - u + 1
            held = tables_ref[places[u], :, block * LANES : (block + 1) * LANES]
            total = total + held.astype(F32)
        totals.append(total)
    scaled = jnp.dot(
        jnp.concatenate(totals, axis=0), mix_ref[...], precision=HIGHEST,
        preferred_element_type=F32,
    )
    scaled = jnp.concatenate(
        [scaled[s * band_pad : (s + 1) * band_pad] for s in range(3)], axis=1
    )
    high = scaled.astype(BF16)
    low = (scaled - high.astype(F32)).astype(BF16)
    sorted_back = dot(jnp.concatenate([high, low], axis=0), sort_ref[...])
    half = sorted_back[:band_pad]
    coef_ref[...] = half + sorted_back[band_pad:]

    acc_ref[...] = jnp.zeros_like(acc_ref)
    group = LANES // proj_count
    for start in range(0, entry_count, group):
        count = min(group, entry_count - start)
        width = count * proj_count
        first = start * proj_count
        held = jnp.broadcast_to(half[:, first : first + width][None], (count, band_pad, width))
        lane = lax.broadcasted_iota(jnp.int32, (count, band_pad, width), 2) // proj_count
        item = lax.broadcasted_iota(jnp.int32, (count, band_pad, width), 0)
        spread = jnp.where(lane == item, held, 0.0).reshape(count * band_pad, width).astype(BF16)
        for j in range(depth):
            terms = dot(spread, proj_ref[first : first + width, j * LANES : (j + 1) * LANES])
            for k in range(count):
                row = rows_ref[start + k] + j
                acc_ref[row] += terms[k * band_pad : (k + 1) * band_pad]

    def turn_back(step, carry):
        rows = pl.ds(pl.multiple_of(step * ROWS, ROWS), ROWS)
        for x in range(0, plane_count, 2):
            blocks = [
                (acc_ref[pl.ds((x + k) * width_y + step * ROWS, ROWS)] * -24.0)
                .astype(BF16)
                .reshape(ROWS * band_pad, LANES)
                for k in range(2)
            ]
            moved = turn_pair(back_ref[...], *blocks)
            for k in range(2):
                part_ref[:, x + k, rows, :] = moved[:, k * LANES : (k + 1) * LANES].reshape(
                    band_count, ROWS, LANES
                )
        return carry

    lax.fori_loop(0, width_y // ROWS, turn_back, 0)
    scale_ref[...] = (pot_ref[...] * -24.0).astype(BF16)

    def inner_copy(b):
        return pltpu.make_async_copy(
            inner_buf.at[b], out_ref.at[b, pl.ds(2, plane_count - 4)], inner_sem.at[b]
        )

    def edge_copy(b):
        return pltpu.make_async_copy(edge_buf.at[b], edge_ref.at[b], edge_sem.at[b])

    def each_pair(pair, carry):
        for x in range(plane_count):
            tops, adds = [], []
            for k in range(2):
                b = pair * 2 + k

                def near(offset):
                    return [
                        wave_ref[b, x + o]
                        for o in (offset, -offset)
                        if 0 <= x + o < plane_count
                    ]

                here = wave_ref[b, x]
                one, two = near(1), near(2)
                side = sum(one[1:], one[0]) * jnp.asarray(16.0, BF16)
                side = side - sum(two[1:], two[0])
                adds.append(side + (scale_ref[x] * here + part_ref[b, x]))
                tops.append(here)
            both = jnp.concatenate(
                [jnp.concatenate(tops, axis=1), jnp.concatenate(adds, axis=1)], axis=0
            )
            lap = dot(second_y_ref[...], both)
            along_z = dot(jnp.concatenate(tops, axis=0), second_z_ref[...])
            for k in range(2):
                b = pair * 2 + k
                total = lap[:, k * LANES : (k + 1) * LANES]
                total = total + along_z[k * width_y : (k + 1) * width_y]
                total = total * (-1.0 / 24.0)
                if x < 2:
                    edge_buf[b, x] = total
                elif x >= plane_count - 2:
                    edge_buf[b, x - plane_count + 4] = total
                else:
                    inner_buf[b, x - 2] = total.astype(BF16)
        for k in range(2):
            inner_copy(pair * 2 + k).start()
            edge_copy(pair * 2 + k).start()
        return carry

    lax.fori_loop(0, band_count // 2, each_pair, 0)

    def finish(b, carry):
        inner_copy(b).wait()
        edge_copy(b).wait()
        return carry

    lax.fori_loop(0, band_count, finish, 0)


def force_kernel(
    dims, dom_count, band_devices, before_ref, after_ref, proj_ref, rows_ref, swap_ref, meas_ref,
    coef_ref, weight_ref, pick_ref, out_ref, field_ref, lhs_ref, extra_ref, part_ref, held_ref,
    send_sem, recv_sem,
):
    band_count, band_pad, plane_count, width_y, entry_count, proj_count, depth = dims
    group = LANES // proj_count
    own = lax.axis_index("dom")
    band = lax.axis_index("band")
    partners = [
        (s, t) for t in range(band_devices) for s in (-1, 0, 1) if (s, t) != (0, 0)
    ]

    def device(s, t):
        return {
            "dom": lax.rem(own + s + dom_count, dom_count),
            "band": lax.rem(band + t, band_devices),
        }

    signal_all([device(s, t) for s, t in partners])

    inner = (plane_count - 4) * width_y
    field_ref[2 * width_y : 2 * width_y + inner] = jnp.zeros((inner, band_pad, LANES), BF16)

    def step_rows(step, carry):
        rows = pl.ds(pl.multiple_of(step * ROWS, ROWS), ROWS)
        b2 = before_ref[:, 0, rows, :].astype(F32)
        b1 = before_ref[:, 1, rows, :].astype(F32)
        a1 = after_ref[:, 0, rows, :].astype(F32)
        a2 = after_ref[:, 1, rows, :].astype(F32)
        last = plane_count - 1
        for x, left, right in ((0, b2 - 8.0 * b1, b1), (last - 1, -a1, 8.0 * a1 - a2)):
            moved = turn_pair(
                swap_ref[...],
                *[
                    (value * (1.0 / 12.0)).astype(BF16).reshape(band_count * ROWS, LANES)
                    for value in (left, right)
                ],
            )
            for k in range(2):
                field_ref[pl.ds((x + k) * width_y + step * ROWS, ROWS)] = moved[
                    :, k * LANES : (k + 1) * LANES
                ].reshape(ROWS, band_pad, LANES)
        return carry

    lax.fori_loop(0, width_y // ROWS, step_rows, 0)
    extra_ref[...] = jnp.zeros_like(extra_ref)
    for start in range(0, entry_count, group):
        count = min(group, entry_count - start)
        width = count * proj_count
        first = start * proj_count

        def fetch(k, carry):
            tile = field_ref[pl.ds(rows_ref[start + k], depth)]
            for j in range(depth):
                lhs_ref[k, :, j * LANES : (j + 1) * LANES] = tile[j]
            return carry

        lax.fori_loop(0, count, fetch, 0)
        lhs = lhs_ref[:count].reshape(count * band_pad, depth * LANES)
        whole = dot_nt(lhs, proj_ref[first : first + width])
        extra_ref[:, first : first + width] = pick_groups(whole, count, band_pad, proj_count)

    weighted = coef_ref[...] * weight_ref[...]
    sums = []
    for k in range(3):
        held = meas_ref[k * band_pad : (k + 1) * band_pad]
        if k == 0:
            held = held + extra_ref[...]
        sums.append(jnp.sum(weighted * held, axis=0, keepdims=True))
    sums = jnp.concatenate(sums + [jnp.zeros((5, sums[0].shape[1]), F32)], axis=0)
    high = sums.astype(BF16)
    rest = sums - high.astype(F32)
    middle = rest.astype(BF16)
    low = (rest - middle.astype(F32)).astype(BF16)
    pieces = jnp.concatenate([high, middle, low, jnp.zeros_like(low)], axis=0)
    spread = dot(pieces, pick_ref[...])
    spread = spread[:8] + spread[8:16] + spread[16:24]
    for s in range(3):
        part_ref[s] = spread[:, s * LANES : (s + 1) * LANES]

    wait_all(partners)
    copies = []
    for s, t in partners:
        slot = (s + 1) * band_devices + t
        copy = pltpu.make_async_remote_copy(
            src_ref=part_ref.at[s + 1],
            dst_ref=held_ref.at[slot],
            send_sem=send_sem.at[slot],
            recv_sem=recv_sem.at[slot],
            device_id=device(s, t),
            device_id_type=pl.DeviceIdType.MESH,
        )
        copy.start()
        copies.append((slot, copy))
    total = part_ref[1]
    for slot, copy in copies:
        copy.wait_recv()
        total = total + held_ref[slot]
    for slot, copy in copies:
        copy.wait_send()
    out_ref[...] = total


def edge_kernel(edge_ref, before_ref, after_ref, inner_ref, out_ref):
    side = pl.program_id(1)

    @pl.when(side == 0)
    def _():
        b2 = before_ref[:, 0].astype(F32)
        b1 = before_ref[:, 1].astype(F32)
        out_ref[:, 0] = (edge_ref[:, 0] + (b2 - 16.0 * b1) * (1.0 / 24.0)).astype(BF16)
        out_ref[:, 1] = (edge_ref[:, 1] + b1 * (1.0 / 24.0)).astype(BF16)

    @pl.when(side == 1)
    def _():
        a1 = after_ref[:, 0].astype(F32)
        a2 = after_ref[:, 1].astype(F32)
        out_ref[:, 0] = (edge_ref[:, 0] + a1 * (1.0 / 24.0)).astype(BF16)
        out_ref[:, 1] = (edge_ref[:, 1] + (a2 - 16.0 * a1) * (1.0 / 24.0)).astype(BF16)


def per_device(
    wavefunctions, potential, projectors, margin_atoms, tile_rows, coupling, band_weights
):
    band_count, plane_count, width_y, width_z = wavefunctions.shape
    entry_count, proj_count, tile_len = projectors.shape
    depth = tile_len // width_z
    row_count = plane_count * width_y
    band_pad = max(band_count, ROWS)
    dims = (band_count, band_pad, plane_count, width_y, entry_count, proj_count, depth)
    dom_count = lax.axis_size("dom")
    band_devices = lax.axis_size("band")
    own_index = lax.axis_index("dom")

    up = [(i, (i + 1) % dom_count) for i in range(dom_count)]
    down = [(j, i) for i, j in up]
    before = lax.ppermute(wavefunctions[:, plane_count - 2 :], "dom", up)
    after = lax.ppermute(wavefunctions[:, :2], "dom", down)

    params = pltpu.CompilerParams(vmem_limit_bytes=VMEM_LIMIT)
    swap = jnp.asarray(band_swap(band_count, band_pad), BF16)
    back = jnp.asarray(band_swap(band_count, band_pad).T, BF16)
    first_z = jnp.asarray(circulant(width_z, {-2: 1.0, -1: -8.0, 1: 8.0, 2: -1.0}), BF16)
    second_z = jnp.asarray(
        circulant(width_z, {-2: -1.0, -1: 16.0, 0: -90.0, 1: 16.0, 2: -1.0}), BF16
    )
    second_y = circulant(width_y, {-2: -1.0, -1: 16.0, 1: 16.0, 2: -1.0})
    second_y = jnp.asarray(
        np.concatenate([second_y, np.eye(width_y, dtype=np.float32)], axis=1), BF16
    )

    relative = lax.rem(margin_atoms // ATOM_DEV - own_index + 1 + dom_count, dom_count)
    entry_lanes = -(-entry_count * proj_count // LANES) * LANES
    lane = jnp.arange(entry_lanes, dtype=jnp.int32)
    spare = (0, entry_lanes // proj_count - entry_count)
    first_lane = jnp.pad(
        relative * LANES + (margin_atoms % ATOM_DEV) * proj_count, spare, constant_values=-LANES
    )
    pick_lane = jnp.pad(
        relative * LANES + margin_atoms % ATOM_DEV, spare, constant_values=-LANES
    )
    target = jnp.arange(3 * LANES, dtype=jnp.int32)[None, :]
    first_lane = jnp.repeat(first_lane, proj_count) + lane % proj_count
    sort = (first_lane[:, None] == target).astype(BF16)
    sort_back = (target.T == first_lane[None, :]).astype(BF16)
    pick = (jnp.repeat(pick_lane, proj_count)[:, None] == target).astype(BF16)
    symmetric = 0.5 * (coupling + coupling.T)
    mix = jnp.kron(jnp.eye(LANES // proj_count, dtype=F32), symmetric)
    weights = jnp.pad(-2.0 * band_weights, (0, band_pad - band_count))[:, None]
    flat = projectors.reshape(entry_count * proj_count, tile_len)
    group = LANES // proj_count

    moves = other_moves(dom_count)
    count = len(moves)
    any_space = pl.BlockSpec(memory_space=pl.ANY)
    tables, measured = pl.pallas_call(
        functools.partial(margin_kernel, dims, dom_count),
        out_shape=(
            jax.ShapeDtypeStruct((count + 1, band_pad, 3 * LANES), BF16),
            jax.ShapeDtypeStruct((3 * band_pad, entry_lanes), F32),
        ),
        in_specs=[vmem(), vmem(), smem(), vmem(), vmem(), vmem()],
        out_specs=(vmem(), vmem()),
        scratch_shapes=[
            pltpu.VMEM(((plane_count + 4) * (width_y + 4), band_pad, width_z), BF16),
            pltpu.VMEM((entry_count * proj_count, tile_len), BF16),
            pltpu.VMEM((group, 2 * band_pad, tile_len), BF16),
            pltpu.VMEM((band_pad, entry_lanes), F32),
            pltpu.VMEM((band_pad, 3 * LANES), BF16),
            pltpu.VMEM((count, band_pad, 3 * LANES), BF16),
            pltpu.SemaphoreType.DMA((count,)),
            pltpu.SemaphoreType.DMA((count,)),
        ],
        compiler_params=pltpu.CompilerParams(
            vmem_limit_bytes=VMEM_LIMIT, collective_id=1, has_side_effects=True
        ),
        cost_estimate=SMALL,
        name="margins",
    )(wavefunctions, flat, tile_rows, swap, sort, first_z)

    places = {u: 0 if u % dom_count == 0 else moves.index(u % dom_count) + 1 for u in range(-2, 3)}
    inner, edge, coef = pl.pallas_call(
        functools.partial(apply_kernel, dims, places),
        out_shape=(
            jax.ShapeDtypeStruct(wavefunctions.shape, BF16),
            jax.ShapeDtypeStruct((band_count, 4, width_y, width_z), F32),
            jax.ShapeDtypeStruct((band_pad, entry_lanes), F32),
        ),
        in_specs=[vmem(), vmem(), vmem(), vmem(), smem()] + [vmem()] * 5,
        out_specs=(any_space, any_space, vmem()),
        scratch_shapes=[
            pltpu.VMEM((row_count, band_pad, width_z), F32),
            pltpu.VMEM(wavefunctions.shape, BF16),
            pltpu.VMEM((plane_count, width_y, width_z), BF16),
            pltpu.VMEM((band_count, plane_count - 4, width_y, width_z), BF16),
            pltpu.VMEM((band_count, 4, width_y, width_z), F32),
            pltpu.SemaphoreType.DMA((band_count,)),
            pltpu.SemaphoreType.DMA((band_count,)),
        ],
        compiler_params=params,
        cost_estimate=SMALL,
        name="apply",
    )(
        tables, wavefunctions, potential, flat, tile_rows, back, sort_back, mix, second_y,
        second_z,
    )

    slots = 3 * band_devices
    forces = pl.pallas_call(
        functools.partial(force_kernel, dims, dom_count, band_devices),
        out_shape=jax.ShapeDtypeStruct((8, LANES), F32),
        in_specs=[vmem(), vmem(), vmem(), smem()] + [vmem()] * 5,
        out_specs=vmem(),
        scratch_shapes=[
            pltpu.VMEM((row_count, band_pad, width_z), BF16),
            pltpu.VMEM((group, band_pad, tile_len), BF16),
            pltpu.VMEM((band_pad, entry_lanes), F32),
            pltpu.VMEM((3, 8, LANES), F32),
            pltpu.VMEM((slots, 8, LANES), F32),
            pltpu.SemaphoreType.DMA((slots,)),
            pltpu.SemaphoreType.DMA((slots,)),
        ],
        compiler_params=pltpu.CompilerParams(
            vmem_limit_bytes=VMEM_LIMIT, collective_id=0, has_side_effects=True
        ),
        cost_estimate=SMALL,
        name="force_sum",
    )(before, after, flat, tile_rows, swap, measured, coef, weights, pick)[:3, :ATOM_DEV]

    chunk = max(band_count // 4, 1)
    applied = pl.pallas_call(
        edge_kernel,
        grid=(band_count // chunk, 2),
        out_shape=jax.ShapeDtypeStruct(wavefunctions.shape, BF16),
        in_specs=[
            pl.BlockSpec((chunk, 2, width_y, width_z), lambda i, side: (i, side, 0, 0)),
            pl.BlockSpec((chunk, 2, width_y, width_z), lambda i, side: (i, 0, 0, 0)),
            pl.BlockSpec((chunk, 2, width_y, width_z), lambda i, side: (i, 0, 0, 0)),
            pl.BlockSpec(memory_space=pl.ANY),
        ],
        out_specs=pl.BlockSpec(
            (chunk, 2, width_y, width_z),
            lambda i, side: (i, side * (plane_count // 2 - 1), 0, 0),
        ),
        input_output_aliases={3: 0},
        compiler_params=params,
        cost_estimate=SMALL,
        name="edges",
    )(edge, before, after, inner)
    return (applied, forces)


def other_moves(dom_count):
    return sorted({u % dom_count for u in range(-2, 3)} - {0})


def solution(mesh):
    placed = (
        P("band", "dom", None, None),
        P("dom", None, None),
        P("dom", None, None),
        P("dom"),
        P("dom"),
        P(),
        P("band"),
    )
    return jax.shard_map(
        per_device,
        mesh=mesh,
        in_specs=placed,
        out_specs=(P("band", "dom", None, None), P(None, "dom")),
        check_vma=False,
    )
```

```python
import functools

import jax
import jax.numpy as jnp
import numpy as np
from jax import lax
from jax.experimental import pallas as pl
from jax.experimental.pallas import tpu as pltpu
from jax.sharding import PartitionSpec as P

ATOM_DEV = 12
LANES = 128
ROWS = 16
VMEM_LIMIT = 52 * 1024 * 1024
F32 = jnp.float32
BF16 = jnp.bfloat16
HIGHEST = lax.Precision.HIGHEST


def vmem():
    return pl.BlockSpec(memory_space=pltpu.VMEM)


def smem():
    return pl.BlockSpec(memory_space=pltpu.SMEM)


def dot(a, b):
    return jnp.dot(a, b, preferred_element_type=F32)


def dot_nt(a, b, precision=None):
    return lax.dot_general(
        a, b, (((1,), (1,)), ((), ())), precision=precision, preferred_element_type=F32
    )


def circulant(width, taps):
    table = np.zeros((width, width), np.float32)
    for offset, value in taps.items():
        for target in range(width):
            table[(target + offset) % width, target] += value
    return table


def band_swap(band_count, band_pad):
    table = np.zeros((ROWS * band_pad, band_count * ROWS), np.float32)
    for y in range(ROWS):
        for b in range(band_count):
            table[y * band_pad + b, b * ROWS + y] = 1.0
    return table


def pick_groups(whole, count, height, proj_count):
    width = count * proj_count
    whole = whole.reshape(count, height, width)
    lane = lax.broadcasted_iota(jnp.int32, (count, height, width), 2) // proj_count
    item = lax.broadcasted_iota(jnp.int32, (count, height, width), 0)
    return jnp.sum(jnp.where(lane == item, whole, 0.0), axis=0)


def turn_pair(swap, left, right):
    return dot(swap, jnp.concatenate([left, right], axis=1)).astype(BF16)


def signal_all(devices):
    barrier = pltpu.get_barrier_semaphore()
    for device in devices:
        pl.semaphore_signal(
            barrier, inc=1, device_id=device, device_id_type=pl.DeviceIdType.MESH
        )


def wait_all(devices):
    pl.semaphore_wait(pltpu.get_barrier_semaphore(), len(devices))


def iota(shape, axis):
    return lax.broadcasted_iota(jnp.int32, shape, axis)


def remote(src, dst, send, recv, device):
    return pltpu.make_async_remote_copy(
        src_ref=src, dst_ref=dst, send_sem=send, recv_sem=recv, device_id=device,
        device_id_type=pl.DeviceIdType.MESH,
    )


def whole_kernel(
    dims, dom_count, band_devices, places, wave_hbm, pot_ref, proj_ref, atoms_ref, rows_ref,
    row_ref, coupling_ref, weight_ref, swap_ref, first_ref, second_y_ref, second_z_ref,
    out_ref, force_ref, wave_ref, halo_ref, turned_ref, proj_z_ref, lhs_ref, margin_ref, meas_ref,
    sort_ref, pick_ref, hit_ref, own_ref, table_ref, term_ref, part_ref, scale_ref, edge_ref,
    field_ref, extra_ref, sums_ref, held_ref, load_sem, halo_send, halo_recv, table_send,
    table_recv, force_send, force_recv,
):
    band_count, band_pad, plane_count, width_y, entry_count, proj_count, depth = dims
    stride = width_y + 4
    row_count = plane_count * width_y
    group = LANES // proj_count
    lanes = meas_ref.shape[1]
    own = lax.axis_index("dom")
    band = lax.axis_index("band")
    moves = other_moves(dom_count)
    partners = [
        (s, t) for t in range(band_devices) for s in (-1, 0, 1) if (s, t) != (0, 0)
    ]

    def device(s, t):
        return {
            "dom": lax.rem(own + s + dom_count, dom_count),
            "band": lax.rem(band + t, band_devices),
        }

    greeted = sorted({(s % dom_count, t) for s, t in partners} | {(u, 0) for u in moves})
    signal_all([device(s, t) for s, t in greeted])
    load = pltpu.make_async_copy(wave_hbm, wave_ref, load_sem)
    load.start()

    turned_ref[: 2 * stride] = jnp.zeros((2 * stride, band_pad, LANES), BF16)
    turned_ref[(plane_count + 2) * stride :] = jnp.zeros((2 * stride, band_pad, LANES), BF16)
    inner = (plane_count - 4) * width_y
    wait_all(greeted)

    halos = [
        remote(
            wave_hbm.at[:, pl.ds(plane_count - 2, 2)], halo_ref.at[0], halo_send.at[0],
            halo_recv.at[0], device(1, 0),
        ),
        remote(
            wave_hbm.at[:, pl.ds(0, 2)], halo_ref.at[1], halo_send.at[1], halo_recv.at[1],
            device(-1, 0),
        ),
    ]
    for copy in halos:
        copy.start()

    field_ref[2 * width_y : 2 * width_y + inner] = jnp.zeros((inner, band_pad, LANES), BF16)
    atoms = atoms_ref[...]
    owner = jnp.zeros_like(atoms)
    for k in range(1, dom_count):
        owner = owner + (atoms >= k * ATOM_DEV).astype(jnp.int32)
    within = atoms - owner * ATOM_DEV
    relative = owner - own + 1
    relative = jnp.where(relative < 0, relative + dom_count, relative)
    relative = jnp.where(relative >= dom_count, relative - dom_count, relative)
    target = iota((entry_count, 3 * LANES), 1)
    first_lane = relative * LANES + within * proj_count
    shift = target - first_lane
    near = ((shift >= 0) & (shift < proj_count)).astype(F32).astype(BF16)
    chosen = (target == relative * LANES + within).astype(F32).astype(BF16)
    entry_of = (iota((lanes, entry_count), 0) // proj_count == iota((lanes, entry_count), 1))
    entry_of = entry_of.astype(F32).astype(BF16)
    square = (lanes, 3 * LANES)
    same = iota(square, 0) % proj_count == iota(square, 1) % proj_count
    sort_ref[...] = jnp.where(same, dot(entry_of, near), 0.0).astype(BF16)
    pick_ref[...] = dot(entry_of, chosen).astype(BF16)
    spots = row_ref.shape[1]
    column = iota((spots, depth * spots), 1)
    entry = (column // LANES) * group + column % group
    entry_at = (entry == iota((spots, depth * spots), 0)).astype(F32)
    goal = jnp.dot(
        jnp.broadcast_to(row_ref[...], (8, spots)), entry_at, precision=HIGHEST,
        preferred_element_type=F32,
    )[:1]
    goal = goal + ((iota(goal.shape, 1) % LANES) // group).astype(F32)
    for x in range(plane_count):
        grid_row = (iota((width_y, depth * spots), 0) + x * width_y).astype(F32)
        hit_ref[x * width_y : (x + 1) * width_y] = (grid_row == goal).astype(F32).astype(BF16)
    scale_ref[...] = (pot_ref[...] * -24.0).astype(BF16)
    for j in range(depth):
        columns = slice(j * LANES, (j + 1) * LANES)
        proj_z_ref[:, columns] = (
            dot(proj_ref[:, columns], first_ref[...]) * (-1.0 / 12.0)
        ).astype(BF16)
    meas_ref[...] = jnp.zeros_like(meas_ref)
    margin_ref[...] = jnp.zeros_like(margin_ref)
    extra_ref[...] = jnp.zeros_like(extra_ref)
    load.wait()

    def turn(step, carry):
        rows = pl.ds(pl.multiple_of(step * ROWS, ROWS), ROWS)
        for x in range(0, plane_count, 2):
            moved = turn_pair(
                swap_ref[...],
                wave_ref[:, x, rows, :].reshape(band_count * ROWS, LANES),
                wave_ref[:, x + 1, rows, :].reshape(band_count * ROWS, LANES),
            )
            for k in range(2):
                turned_ref[pl.ds((x + k + 2) * stride + 2 + step * ROWS, ROWS)] = moved[
                    :, k * LANES : (k + 1) * LANES
                ].reshape(ROWS, band_pad, LANES)
        return carry

    lax.fori_loop(0, width_y // ROWS, turn, 0)
    for x in range(2, plane_count + 2):
        base = x * stride
        turned_ref[base : base + 2] = turned_ref[base + width_y : base + width_y + 2]
        turned_ref[base + width_y + 2 : base + width_y + 4] = turned_ref[base + 2 : base + 4]

    bits = width_y.bit_length() - 1

    def place(row, j):
        at = row + j
        return at + 4 * lax.shift_right_logical(at, bits) + 2 * stride + 2

    def each_group(body, height, weight_list):
        for start in range(0, entry_count, group):
            count = min(group, entry_count - start)
            width = count * proj_count
            first = start * proj_count
            lax.fori_loop(0, count, functools.partial(body, start), 0, unroll=4)
            lhs = lhs_ref[:count, :height].reshape(count * height, depth * LANES)
            for weight_ref_, result_ref, low in weight_list:
                whole = dot_nt(lhs, weight_ref_[first : first + width])
                result_ref[low : low + height, first : first + width] = pick_groups(
                    whole, count, height, proj_count
                )

    def fetch(start, k, carry):
        row = rows_ref[start + k]
        for j in range(depth):
            lhs_ref[k, :band_pad, j * LANES : (j + 1) * LANES] = turned_ref[place(row, j)]
        return carry

    each_group(fetch, band_pad, [(proj_ref, margin_ref, 0), (proj_z_ref, meas_ref, 2 * band_pad)])
    own_ref[...] = dot(margin_ref[...].astype(BF16), sort_ref[...]).astype(BF16)
    copies = []
    for slot, u in enumerate(moves):
        copy = remote(
            own_ref, table_ref.at[slot], table_send.at[slot], table_recv.at[slot], device(-u, 0)
        )
        copy.start()
        copies.append(copy)

    def derive(start, k, carry):
        row = rows_ref[start + k]
        for j in range(depth):
            at = place(row, j)
            columns = slice(j * LANES, (j + 1) * LANES)
            for part, step in ((0, stride), (1, 1)):
                far = turned_ref[at - 2 * step].astype(F32) - turned_ref[at + 2 * step].astype(F32)
                side = turned_ref[at + step].astype(F32) - turned_ref[at - step].astype(F32)
                lhs_ref[k, part * band_pad : (part + 1) * band_pad, columns] = (
                    far * (1.0 / 12.0) + side * (2.0 / 3.0)
                ).astype(BF16)
        return carry

    each_group(derive, 2 * band_pad, [(proj_ref, meas_ref, 0)])

    for copy in copies:
        copy.wait_recv()
    tables = [own_ref[...]] + [table_ref[slot] for slot in range(len(moves))]
    totals = []
    for s in (-1, 0, 1):
        total = jnp.zeros((band_pad, LANES), F32)
        for u in (s - 1, s, s + 1):
            block = s - u + 1
            total = total + tables[places[u]][:, block * LANES : (block + 1) * LANES].astype(F32)
        totals.append(total)
    inside = (iota((LANES, proj_count), 0) % proj_count == iota((LANES, proj_count), 1)).astype(F32)
    spread = jnp.dot(inside, coupling_ref[...], precision=HIGHEST, preferred_element_type=F32)
    mix = 0.5 * (dot_nt(spread, inside, HIGHEST) + dot_nt(inside, spread, HIGHEST))
    square = (LANES, LANES)
    mix = jnp.where(
        iota(square, 0) // proj_count == iota(square, 1) // proj_count, mix, 0.0
    )
    scaled = jnp.dot(
        jnp.concatenate(totals, axis=0), mix, precision=HIGHEST, preferred_element_type=F32
    )
    scaled = jnp.concatenate(
        [scaled[s * band_pad : (s + 1) * band_pad] for s in range(3)], axis=1
    )
    high = scaled.astype(BF16)
    low = (scaled - high.astype(F32)).astype(BF16)
    sorted_back = dot_nt(jnp.concatenate([high, low], axis=0), sort_ref[...])
    half = sorted_back[:band_pad]
    weighted = (half + sorted_back[band_pad:]) * weight_ref[...]

    for index, start in enumerate(range(0, entry_count, group)):
        width = min(group, entry_count - start) * proj_count
        first = start * proj_count
        shape = (band_pad, group, width)
        held = jnp.broadcast_to(half[:, first : first + width][:, None], shape)
        held = jnp.where(iota(shape, 2) // proj_count == iota(shape, 1), held, 0.0)
        held = held.reshape(band_pad * group, width).astype(BF16)
        for j in range(depth):
            terms = dot(held, proj_ref[first : first + width, j * LANES : (j + 1) * LANES])
            at = index * LANES + j * group
            term_ref[:, at : at + group, :] = (
                (terms * -24.0).astype(BF16).reshape(band_pad, group, LANES)
            )

    def each_pair(pair, carry):
        terms = jnp.concatenate([term_ref[pair * 2], term_ref[pair * 2 + 1]], axis=1)
        part_ref[...] = dot(hit_ref[...], terms).astype(BF16)
        for x in range(plane_count):
            tops, adds = [], []
            for k in range(2):
                b = pair * 2 + k

                def near(offset):
                    return [
                        wave_ref[b, x + o]
                        for o in (offset, -offset)
                        if 0 <= x + o < plane_count
                    ]

                here = wave_ref[b, x]
                one, two = near(1), near(2)
                side = sum(one[1:], one[0]) * jnp.asarray(16.0, BF16)
                side = side - sum(two[1:], two[0])
                part = part_ref[x * width_y : (x + 1) * width_y, k * LANES : (k + 1) * LANES]
                adds.append(side + (scale_ref[x] * here + part))
                tops.append(here)
            both = jnp.concatenate(
                [jnp.concatenate(tops, axis=1), jnp.concatenate(adds, axis=1)], axis=0
            )
            lap = dot(second_y_ref[...], both)
            along_z = dot(jnp.concatenate(tops, axis=0), second_z_ref[...])
            for k in range(2):
                b = pair * 2 + k
                total = lap[:, k * LANES : (k + 1) * LANES]
                total = total + along_z[k * width_y : (k + 1) * width_y]
                total = total * (-1.0 / 24.0)
                if x < 2:
                    edge_ref[b, x] = total
                elif x >= plane_count - 2:
                    edge_ref[b, x - plane_count + 4] = total
                else:
                    out_ref[b, x] = total.astype(BF16)
        return carry

    lax.fori_loop(0, band_count // 2, each_pair, 0)

    for copy in halos:
        copy.wait_recv()

    def halo_rows(step, carry):
        rows = pl.ds(pl.multiple_of(step * ROWS, ROWS), ROWS)
        b2 = halo_ref[0, :, 0, rows, :].astype(F32)
        b1 = halo_ref[0, :, 1, rows, :].astype(F32)
        a1 = halo_ref[1, :, 0, rows, :].astype(F32)
        a2 = halo_ref[1, :, 1, rows, :].astype(F32)
        last = plane_count - 1
        for x, left, right in ((0, b2 - 8.0 * b1, b1), (last - 1, -a1, 8.0 * a1 - a2)):
            moved = turn_pair(
                swap_ref[...],
                *[
                    (value * (1.0 / 12.0)).astype(BF16).reshape(band_count * ROWS, LANES)
                    for value in (left, right)
                ],
            )
            for k in range(2):
                field_ref[pl.ds((x + k) * width_y + step * ROWS, ROWS)] = moved[
                    :, k * LANES : (k + 1) * LANES
                ].reshape(ROWS, band_pad, LANES)
        return carry

    lax.fori_loop(0, width_y // ROWS, halo_rows, 0)

    def fetch_halo(start, k, carry):
        tile = field_ref[pl.ds(rows_ref[start + k], depth)]
        for j in range(depth):
            lhs_ref[k, :band_pad, j * LANES : (j + 1) * LANES] = tile[j]
        return carry

    each_group(fetch_halo, band_pad, [(proj_ref, extra_ref, 0)])
    sums = []
    for k in range(3):
        held = meas_ref[k * band_pad : (k + 1) * band_pad]
        if k == 0:
            held = held + extra_ref[...]
        sums.append(jnp.sum(weighted * held, axis=0, keepdims=True))
    sums = jnp.concatenate(sums + [jnp.zeros((5, lanes), F32)], axis=0)
    high = sums.astype(BF16)
    rest = sums - high.astype(F32)
    middle = rest.astype(BF16)
    low = (rest - middle.astype(F32)).astype(BF16)
    pieces = jnp.concatenate([high, middle, low, jnp.zeros_like(low)], axis=0)
    spread = dot(pieces, pick_ref[...])
    spread = spread[:8] + spread[8:16] + spread[16:24]
    for s in range(3):
        sums_ref[s] = spread[:, s * LANES : (s + 1) * LANES]
    force_copies = []
    for s, t in partners:
        slot = (s + 1) * band_devices + t
        copy = remote(
            sums_ref.at[s + 1], held_ref.at[slot], force_send.at[slot], force_recv.at[slot],
            device(s, t),
        )
        copy.start()
        force_copies.append((slot, copy))

    def edges(b, carry):
        b2 = halo_ref[0, b, 0].astype(F32)
        b1 = halo_ref[0, b, 1].astype(F32)
        a1 = halo_ref[1, b, 0].astype(F32)
        a2 = halo_ref[1, b, 1].astype(F32)
        last = plane_count - 1
        share = 1.0 / 24.0
        out_ref[b, 0] = (edge_ref[b, 0] + (b2 - 16.0 * b1) * share).astype(BF16)
        out_ref[b, 1] = (edge_ref[b, 1] + b1 * share).astype(BF16)
        out_ref[b, last - 1] = (edge_ref[b, 2] + a1 * share).astype(BF16)
        out_ref[b, last] = (edge_ref[b, 3] + (a2 - 16.0 * a1) * share).astype(BF16)
        return carry

    lax.fori_loop(0, band_count, edges, 0)
    total = sums_ref[1]
    for slot, copy in force_copies:
        copy.wait_recv()
        total = total + held_ref[slot]
    force_ref[...] = total
    for copy in halos + copies + [copy for _, copy in force_copies]:
        copy.wait_send()


def per_device(
    wavefunctions, potential, projectors, margin_atoms, tile_rows, coupling, band_weights
):
    band_count, plane_count, width_y, width_z = wavefunctions.shape
    entry_count, proj_count, tile_len = projectors.shape
    depth = tile_len // width_z
    row_count = plane_count * width_y
    band_pad = max(band_count, ROWS)
    dims = (band_count, band_pad, plane_count, width_y, entry_count, proj_count, depth)
    dom_count = lax.axis_size("dom")
    band_devices = lax.axis_size("band")
    group = LANES // proj_count
    lanes = -(-entry_count * proj_count // LANES) * LANES
    spots = lanes // proj_count

    swap = jnp.asarray(band_swap(band_count, band_pad), BF16)
    first_z = jnp.asarray(circulant(width_z, {-2: 1.0, -1: -8.0, 1: 8.0, 2: -1.0}), BF16)
    second_z = jnp.asarray(
        circulant(width_z, {-2: -1.0, -1: 16.0, 0: -90.0, 1: 16.0, 2: -1.0}), BF16
    )
    second_y = circulant(width_y, {-2: -1.0, -1: 16.0, 1: 16.0, 2: -1.0})
    second_y = jnp.asarray(
        np.concatenate([second_y, np.eye(width_y, dtype=np.float32)], axis=1), BF16
    )
    weights = jnp.pad(-2.0 * band_weights, (0, band_pad - band_count))[:, None]
    flat = projectors.reshape(entry_count * proj_count, tile_len)
    row_line = jnp.pad(
        tile_rows.astype(F32), (0, spots - entry_count), constant_values=-4096.0
    )[None]

    moves = other_moves(dom_count)
    places = {u: 0 if u % dom_count == 0 else moves.index(u % dom_count) + 1 for u in range(-2, 3)}
    count = len(moves)
    slots = 3 * band_devices
    applied, forces = pl.pallas_call(
        functools.partial(whole_kernel, dims, dom_count, band_devices, places),
        out_shape=(
            jax.ShapeDtypeStruct(wavefunctions.shape, BF16),
            jax.ShapeDtypeStruct((8, LANES), F32),
        ),
        in_specs=[pl.BlockSpec(memory_space=pl.ANY), vmem(), vmem(), vmem(), smem()]
        + [vmem()] * 7,
        out_specs=(vmem(), vmem()),
        scratch_shapes=[
            pltpu.VMEM(wavefunctions.shape, BF16),
            pltpu.VMEM((2, band_count, 2, width_y, width_z), BF16),
            pltpu.VMEM(((plane_count + 4) * (width_y + 4), band_pad, width_z), BF16),
            pltpu.VMEM((entry_count * proj_count, tile_len), BF16),
            pltpu.VMEM((group, 2 * band_pad, tile_len), BF16),
            pltpu.VMEM((band_pad, lanes), F32),
            pltpu.VMEM((3 * band_pad, lanes), F32),
            pltpu.VMEM((lanes, 3 * LANES), BF16),
            pltpu.VMEM((lanes, 3 * LANES), BF16),
            pltpu.VMEM((row_count, depth * spots), BF16),
            pltpu.VMEM((band_pad, 3 * LANES), BF16),
            pltpu.VMEM((count, band_pad, 3 * LANES), BF16),
            pltpu.VMEM((band_pad, depth * spots, width_z), BF16),
            pltpu.VMEM((row_count, 2 * width_z), BF16),
            pltpu.VMEM((plane_count, width_y, width_z), BF16),
            pltpu.VMEM((band_count, 4, width_y, width_z), F32),
            pltpu.VMEM((row_count, band_pad, width_z), BF16),
            pltpu.VMEM((band_pad, lanes), F32),
            pltpu.VMEM((3, 8, LANES), F32),
            pltpu.VMEM((slots, 8, LANES), F32),
            pltpu.SemaphoreType.DMA,
            pltpu.SemaphoreType.DMA((2,)),
            pltpu.SemaphoreType.DMA((2,)),
            pltpu.SemaphoreType.DMA((count,)),
            pltpu.SemaphoreType.DMA((count,)),
            pltpu.SemaphoreType.DMA((slots,)),
            pltpu.SemaphoreType.DMA((slots,)),
        ],
        compiler_params=pltpu.CompilerParams(
            vmem_limit_bytes=VMEM_LIMIT, collective_id=0, has_side_effects=True
        ),
        cost_estimate=pl.CostEstimate(
            flops=8 << 30, bytes_accessed=10 << 20, transcendentals=0
        ),
        name="step",
    )(
        wavefunctions, potential, flat, margin_atoms[:, None], tile_rows, row_line, coupling,
        weights, swap, first_z, second_y, second_z,
    )
    return (applied, forces[:3, :ATOM_DEV])


def other_moves(dom_count):
    return sorted({u % dom_count for u in range(-2, 3)} - {0})


def solution(mesh):
    placed = (
        P("band", "dom", None, None),
        P("dom", None, None),
        P("dom", None, None),
        P("dom"),
        P("dom"),
        P(),
        P("band"),
    )
    return jax.shard_map(
        per_device,
        mesh=mesh,
        in_specs=placed,
        out_specs=(P("band", "dom", None, None), P(None, "dom")),
        check_vma=False,
    )
```

```python
import functools

import jax
import jax.numpy as jnp
import numpy as np
from jax import lax
from jax.experimental import pallas as pl
from jax.experimental.pallas import tpu as pltpu
from jax.sharding import PartitionSpec as P

ATOM_DEV = 12
LANES = 128
ROWS = 16
VMEM_LIMIT = 62 * 1024 * 1024
F32 = jnp.float32
BF16 = jnp.bfloat16
HIGHEST = lax.Precision.HIGHEST


def vmem():
    return pl.BlockSpec(memory_space=pltpu.VMEM)


def smem():
    return pl.BlockSpec(memory_space=pltpu.SMEM)


def dot(a, b):
    return jnp.dot(a, b, preferred_element_type=F32)


def dot_nt(a, b, precision=None):
    return lax.dot_general(
        a, b, (((1,), (1,)), ((), ())), precision=precision, preferred_element_type=F32
    )


def circulant(width, taps):
    table = np.zeros((width, width), np.float32)
    for offset, value in taps.items():
        for target in range(width):
            table[(target + offset) % width, target] += value
    return table


def band_swap(band_count, band_pad):
    table = np.zeros((ROWS * band_pad, band_count * ROWS), np.float32)
    for y in range(ROWS):
        for b in range(band_count):
            table[y * band_pad + b, b * ROWS + y] = 1.0
    return table


def pick_groups(whole, count, height, proj_count):
    width = count * proj_count
    whole = whole.reshape(count, height, width)
    lane = lax.broadcasted_iota(jnp.int32, (count, height, width), 2) // proj_count
    item = lax.broadcasted_iota(jnp.int32, (count, height, width), 0)
    return jnp.sum(jnp.where(lane == item, whole, 0.0), axis=0)


def turn_pair(swap, left, right):
    return dot(swap, jnp.concatenate([left, right], axis=1)).astype(BF16)


def signal_all(devices):
    barrier = pltpu.get_barrier_semaphore()
    for device in devices:
        pl.semaphore_signal(
            barrier, inc=1, device_id=device, device_id_type=pl.DeviceIdType.MESH
        )


def wait_all(devices):
    pl.semaphore_wait(pltpu.get_barrier_semaphore(), len(devices))


def iota(shape, axis):
    return lax.broadcasted_iota(jnp.int32, shape, axis)


def remote(src, dst, send, recv, device):
    return pltpu.make_async_remote_copy(
        src_ref=src, dst_ref=dst, send_sem=send, recv_sem=recv, device_id=device,
        device_id_type=pl.DeviceIdType.MESH,
    )


def whole_kernel(
    dims, dom_count, band_devices, places, wave_hbm, pot_ref, proj_ref, atoms_ref, rows_ref,
    coupling_ref, weight_ref, swap_ref, first_ref, second_y_ref, second_z_ref,
    out_hbm, force_ref, out_ref, wave_ref, halo_ref, turned_ref, proj_z_ref, lhs_ref, margin_ref, meas_ref,
    sort_ref, pick_ref, hit_ref, own_ref, table_ref, term_ref, part_ref, scale_ref, edge_ref,
    field_ref, extra_ref, sums_ref, held_ref, load_sem, halo_send, halo_recv, table_send,
    table_recv, force_send, force_recv, out_sem,
):
    band_count, band_pad, plane_count, width_y, entry_count, proj_count, depth = dims
    stride = width_y + 4
    row_count = plane_count * width_y
    group = LANES // proj_count
    lanes = meas_ref.shape[1]
    own = lax.axis_index("dom")
    band = lax.axis_index("band")
    moves = other_moves(dom_count)
    partners = [
        (s, t) for t in range(band_devices) for s in (-1, 0, 1) if (s, t) != (0, 0)
    ]

    def device(s, t):
        return {
            "dom": lax.rem(own + s + dom_count, dom_count),
            "band": lax.rem(band + t, band_devices),
        }

    greeted = sorted({(s % dom_count, t) for s, t in partners} | {(u, 0) for u in moves})
    signal_all([device(s, t) for s, t in greeted])
    load = pltpu.make_async_copy(wave_hbm, wave_ref, load_sem)
    load.start()

    turned_ref[: 2 * stride] = jnp.zeros((2 * stride, band_pad, LANES), BF16)
    turned_ref[(plane_count + 2) * stride :] = jnp.zeros((2 * stride, band_pad, LANES), BF16)
    inner = (plane_count - 4) * width_y
    wait_all(greeted)

    halos = [
        remote(
            wave_hbm.at[:, pl.ds(plane_count - 2, 2)], halo_ref.at[0], halo_send.at[0],
            halo_recv.at[0], device(1, 0),
        ),
        remote(
            wave_hbm.at[:, pl.ds(0, 2)], halo_ref.at[1], halo_send.at[1], halo_recv.at[1],
            device(-1, 0),
        ),
    ]
    for copy in halos:
        copy.start()

    field_ref[2 * width_y : 2 * width_y + inner] = jnp.zeros((inner, band_pad, LANES), BF16)
    spots = lanes // proj_count
    slot_of = iota((entry_count, 3 * LANES), 0)
    atoms = jnp.zeros((entry_count, 3 * LANES), jnp.int32)
    line = jnp.full((8, spots), -4096, jnp.int32)
    for e in range(entry_count):
        atoms = jnp.where(slot_of == e, atoms_ref[e], atoms)
        line = jnp.where(iota((8, spots), 1) == e, rows_ref[e], line)
    weight = jnp.zeros((band_pad, lanes), F32)
    for b in range(band_count):
        weight = jnp.where(iota((band_pad, lanes), 0) == b, -2.0 * weight_ref[b], weight)
    owner = jnp.zeros_like(atoms)
    for k in range(1, dom_count):
        owner = owner + (atoms >= k * ATOM_DEV).astype(jnp.int32)
    within = atoms - owner * ATOM_DEV
    relative = owner - own + 1
    relative = jnp.where(relative < 0, relative + dom_count, relative)
    relative = jnp.where(relative >= dom_count, relative - dom_count, relative)
    target = iota((entry_count, 3 * LANES), 1)
    first_lane = relative * LANES + within * proj_count
    shift = target - first_lane
    near = ((shift >= 0) & (shift < proj_count)).astype(F32).astype(BF16)
    chosen = (target == relative * LANES + within).astype(F32).astype(BF16)
    entry_of = (iota((lanes, entry_count), 0) // proj_count == iota((lanes, entry_count), 1))
    entry_of = entry_of.astype(F32).astype(BF16)
    square = (lanes, 3 * LANES)
    same = iota(square, 0) % proj_count == iota(square, 1) % proj_count
    sort_ref[...] = jnp.where(same, dot(entry_of, near), 0.0).astype(BF16)
    pick_ref[...] = dot(entry_of, chosen).astype(BF16)
    column = iota((spots, depth * spots), 1)
    entry = (column // LANES) * group + column % group
    entry_at = (entry == iota((spots, depth * spots), 0)).astype(F32)
    goal = jnp.dot(
        line.astype(F32), entry_at, precision=HIGHEST, preferred_element_type=F32
    )[:1]
    goal = goal + ((iota(goal.shape, 1) % LANES) // group).astype(F32)
    for x in range(plane_count):
        grid_row = (iota((width_y, depth * spots), 0) + x * width_y).astype(F32)
        hit_ref[x * width_y : (x + 1) * width_y] = (grid_row == goal).astype(F32).astype(BF16)
    scale_ref[...] = (pot_ref[...] * -24.0).astype(BF16)
    for j in range(depth):
        columns = slice(j * LANES, (j + 1) * LANES)
        proj_z_ref[:, columns] = (
            dot(proj_ref[:, columns], first_ref[...]) * (-1.0 / 12.0)
        ).astype(BF16)
    meas_ref[...] = jnp.zeros_like(meas_ref)
    margin_ref[...] = jnp.zeros_like(margin_ref)
    extra_ref[...] = jnp.zeros_like(extra_ref)
    load.wait()

    def turn(step, carry):
        rows = pl.ds(pl.multiple_of(step * ROWS, ROWS), ROWS)
        for x in range(0, plane_count, 2):
            moved = turn_pair(
                swap_ref[...],
                wave_ref[:, x, rows, :].reshape(band_count * ROWS, LANES),
                wave_ref[:, x + 1, rows, :].reshape(band_count * ROWS, LANES),
            )
            for k in range(2):
                turned_ref[pl.ds((x + k + 2) * stride + 2 + step * ROWS, ROWS)] = moved[
                    :, k * LANES : (k + 1) * LANES
                ].reshape(ROWS, band_pad, LANES)
        return carry

    lax.fori_loop(0, width_y // ROWS, turn, 0)
    for x in range(2, plane_count + 2):
        base = x * stride
        turned_ref[base : base + 2] = turned_ref[base + width_y : base + width_y + 2]
        turned_ref[base + width_y + 2 : base + width_y + 4] = turned_ref[base + 2 : base + 4]

    bits = width_y.bit_length() - 1

    def place(row, j):
        at = row + j
        return at + 4 * lax.shift_right_logical(at, bits) + 2 * stride + 2

    def each_group(body, height, weight_list):
        for start in range(0, entry_count, group):
            count = min(group, entry_count - start)
            width = count * proj_count
            first = start * proj_count
            lax.fori_loop(0, count, functools.partial(body, start), 0, unroll=4)
            lhs = lhs_ref[:count, :height].reshape(count * height, depth * LANES)
            for weight_ref_, result_ref, low in weight_list:
                whole = dot_nt(lhs, weight_ref_[first : first + width])
                result_ref[low : low + height, first : first + width] = pick_groups(
                    whole, count, height, proj_count
                )

    def fetch(start, k, carry):
        row = rows_ref[start + k]
        for j in range(depth):
            lhs_ref[k, :band_pad, j * LANES : (j + 1) * LANES] = turned_ref[place(row, j)]
        return carry

    each_group(fetch, band_pad, [(proj_ref, margin_ref, 0), (proj_z_ref, meas_ref, 2 * band_pad)])
    own_ref[...] = dot(margin_ref[...].astype(BF16), sort_ref[...]).astype(BF16)
    copies = []
    for slot, u in enumerate(moves):
        copy = remote(
            own_ref, table_ref.at[slot], table_send.at[slot], table_recv.at[slot], device(-u, 0)
        )
        copy.start()
        copies.append(copy)

    def derive(start, k, carry):
        row = rows_ref[start + k]
        for j in range(depth):
            at = place(row, j)
            columns = slice(j * LANES, (j + 1) * LANES)
            for part, step in ((0, stride), (1, 1)):
                far = turned_ref[at - 2 * step].astype(F32) - turned_ref[at + 2 * step].astype(F32)
                side = turned_ref[at + step].astype(F32) - turned_ref[at - step].astype(F32)
                lhs_ref[k, part * band_pad : (part + 1) * band_pad, columns] = (
                    far * (1.0 / 12.0) + side * (2.0 / 3.0)
                ).astype(BF16)
        return carry

    each_group(derive, 2 * band_pad, [(proj_ref, meas_ref, 0)])

    for copy in copies:
        copy.wait_recv()
    tables = [own_ref[...]] + [table_ref[slot] for slot in range(len(moves))]
    totals = []
    for s in (-1, 0, 1):
        total = jnp.zeros((band_pad, LANES), F32)
        for u in (s - 1, s, s + 1):
            block = s - u + 1
            total = total + tables[places[u]][:, block * LANES : (block + 1) * LANES].astype(F32)
        totals.append(total)
    inside = (iota((LANES, proj_count), 0) % proj_count == iota((LANES, proj_count), 1)).astype(F32)
    spread = jnp.dot(inside, coupling_ref[...], precision=HIGHEST, preferred_element_type=F32)
    mix = 0.5 * (dot_nt(spread, inside, HIGHEST) + dot_nt(inside, spread, HIGHEST))
    square = (LANES, LANES)
    mix = jnp.where(
        iota(square, 0) // proj_count == iota(square, 1) // proj_count, mix, 0.0
    )
    scaled = jnp.dot(
        jnp.concatenate(totals, axis=0), mix, precision=HIGHEST, preferred_element_type=F32
    )
    scaled = jnp.concatenate(
        [scaled[s * band_pad : (s + 1) * band_pad] for s in range(3)], axis=1
    )
    high = scaled.astype(BF16)
    low = (scaled - high.astype(F32)).astype(BF16)
    sorted_back = dot_nt(jnp.concatenate([high, low], axis=0), sort_ref[...])
    half = sorted_back[:band_pad]
    weighted = (half + sorted_back[band_pad:]) * weight

    for index, start in enumerate(range(0, entry_count, group)):
        width = min(group, entry_count - start) * proj_count
        first = start * proj_count
        shape = (band_pad, group, width)
        held = jnp.broadcast_to(half[:, first : first + width][:, None], shape)
        held = jnp.where(iota(shape, 2) // proj_count == iota(shape, 1), held, 0.0)
        held = held.reshape(band_pad * group, width).astype(BF16)
        for j in range(depth):
            terms = dot(held, proj_ref[first : first + width, j * LANES : (j + 1) * LANES])
            at = index * LANES + j * group
            term_ref[:, at : at + group, :] = (
                (terms * -24.0).astype(BF16).reshape(band_pad, group, LANES)
            )

    def inner_copy(b):
        planes = pl.ds(2, plane_count - 4)
        return pltpu.make_async_copy(
            out_ref.at[b, planes], out_hbm.at[b, planes], out_sem.at[b]
        )

    def edge_copy(side):
        planes = pl.ds(side * (plane_count - 2), 2)
        return pltpu.make_async_copy(
            out_ref.at[:, planes], out_hbm.at[:, planes], out_sem.at[band_count + side]
        )

    def each_pair(pair, carry):
        terms = jnp.concatenate([term_ref[pair * 2], term_ref[pair * 2 + 1]], axis=1)
        part_ref[...] = dot(hit_ref[...], terms).astype(BF16)
        for x in range(plane_count):
            tops, adds = [], []
            for k in range(2):
                b = pair * 2 + k

                def near(offset):
                    return [
                        wave_ref[b, x + o]
                        for o in (offset, -offset)
                        if 0 <= x + o < plane_count
                    ]

                here = wave_ref[b, x]
                one, two = near(1), near(2)
                side = sum(one[1:], one[0]) * jnp.asarray(16.0, BF16)
                side = side - sum(two[1:], two[0])
                part = part_ref[x * width_y : (x + 1) * width_y, k * LANES : (k + 1) * LANES]
                adds.append(side + (scale_ref[x] * here + part))
                tops.append(here)
            both = jnp.concatenate(
                [jnp.concatenate(tops, axis=1), jnp.concatenate(adds, axis=1)], axis=0
            )
            lap = dot(second_y_ref[...], both)
            along_z = dot(jnp.concatenate(tops, axis=0), second_z_ref[...])
            for k in range(2):
                b = pair * 2 + k
                total = lap[:, k * LANES : (k + 1) * LANES]
                total = total + along_z[k * width_y : (k + 1) * width_y]
                total = total * (-1.0 / 24.0)
                if x < 2:
                    edge_ref[b, x] = total
                elif x >= plane_count - 2:
                    edge_ref[b, x - plane_count + 4] = total
                else:
                    out_ref[b, x] = total.astype(BF16)
        for k in range(2):
            inner_copy(pair * 2 + k).start()
        return carry

    lax.fori_loop(0, band_count // 2, each_pair, 0)

    last = plane_count - 1
    share = 1.0 / 24.0

    def turn_halo(side):
        def halo_rows(step, carry):
            rows = pl.ds(pl.multiple_of(step * ROWS, ROWS), ROWS)
            first = halo_ref[side, :, 0, rows, :].astype(F32)
            second = halo_ref[side, :, 1, rows, :].astype(F32)
            if side == 0:
                x, left, right = 0, first - 8.0 * second, second
            else:
                x, left, right = last - 1, -first, 8.0 * first - second
            moved = turn_pair(
                swap_ref[...],
                *[
                    (value * (1.0 / 12.0)).astype(BF16).reshape(band_count * ROWS, LANES)
                    for value in (left, right)
                ],
            )
            for k in range(2):
                field_ref[pl.ds((x + k) * width_y + step * ROWS, ROWS)] = moved[
                    :, k * LANES : (k + 1) * LANES
                ].reshape(ROWS, band_pad, LANES)
            return carry

        lax.fori_loop(0, width_y // ROWS, halo_rows, 0)

    def edge_side(side):
        def edges(b, carry):
            first = halo_ref[side, b, 0].astype(F32)
            second = halo_ref[side, b, 1].astype(F32)
            if side == 0:
                x, left, right = 0, first - 16.0 * second, second
            else:
                x, left, right = last - 1, first, second - 16.0 * first
            out_ref[b, x] = (edge_ref[b, 2 * side] + left * share).astype(BF16)
            out_ref[b, x + 1] = (edge_ref[b, 2 * side + 1] + right * share).astype(BF16)
            return carry

        lax.fori_loop(0, band_count, edges, 0)
        edge_copy(side).start()

    even = lax.rem(own, 2) == 0

    def on_sides(even_side, body):
        @pl.when(even)
        def _():
            body(even_side)

        @pl.when(jnp.logical_not(even))
        def _():
            body(1 - even_side)

    def near_halo(side):
        halos[side].wait_recv()
        turn_halo(side)
        edge_side(side)

    def far_halo(side):
        halos[side].wait_recv()
        turn_halo(side)

    on_sides(1, near_halo)
    on_sides(0, far_halo)

    def fetch_halo(start, k, carry):
        tile = field_ref[pl.ds(rows_ref[start + k], depth)]
        for j in range(depth):
            lhs_ref[k, :band_pad, j * LANES : (j + 1) * LANES] = tile[j]
        return carry

    each_group(fetch_halo, band_pad, [(proj_ref, extra_ref, 0)])
    sums = []
    for k in range(3):
        held = meas_ref[k * band_pad : (k + 1) * band_pad]
        if k == 0:
            held = held + extra_ref[...]
        sums.append(jnp.sum(weighted * held, axis=0, keepdims=True))
    sums = jnp.concatenate(sums + [jnp.zeros((5, lanes), F32)], axis=0)
    high = sums.astype(BF16)
    rest = sums - high.astype(F32)
    middle = rest.astype(BF16)
    low = (rest - middle.astype(F32)).astype(BF16)
    pieces = jnp.concatenate([high, middle, low, jnp.zeros_like(low)], axis=0)
    spread = dot(pieces, pick_ref[...])
    spread = spread[:8] + spread[8:16] + spread[16:24]
    for s in range(3):
        sums_ref[s] = spread[:, s * LANES : (s + 1) * LANES]
    force_copies = []
    for s, t in partners:
        slot = (s + 1) * band_devices + t
        copy = remote(
            sums_ref.at[s + 1], held_ref.at[slot], force_send.at[slot], force_recv.at[slot],
            device(s, t),
        )
        copy.start()
        force_copies.append((slot, copy))

    on_sides(0, edge_side)
    total = sums_ref[1]
    for slot, copy in force_copies:
        copy.wait_recv()
        total = total + held_ref[slot]
    force_ref[...] = total
    for copy in halos + copies + [copy for _, copy in force_copies]:
        copy.wait_send()

    def finish(b, carry):
        inner_copy(b).wait()
        return carry

    lax.fori_loop(0, band_count, finish, 0)
    for side in range(2):
        edge_copy(side).wait()


def per_device(
    wavefunctions, potential, projectors, margin_atoms, tile_rows, coupling, band_weights
):
    band_count, plane_count, width_y, width_z = wavefunctions.shape
    entry_count, proj_count, tile_len = projectors.shape
    depth = tile_len // width_z
    row_count = plane_count * width_y
    band_pad = max(band_count, ROWS)
    dims = (band_count, band_pad, plane_count, width_y, entry_count, proj_count, depth)
    dom_count = lax.axis_size("dom")
    band_devices = lax.axis_size("band")
    group = LANES // proj_count
    lanes = -(-entry_count * proj_count // LANES) * LANES
    spots = lanes // proj_count

    swap = jnp.asarray(band_swap(band_count, band_pad), BF16)
    first_z = jnp.asarray(circulant(width_z, {-2: 1.0, -1: -8.0, 1: 8.0, 2: -1.0}), BF16)
    second_z = jnp.asarray(
        circulant(width_z, {-2: -1.0, -1: 16.0, 0: -90.0, 1: 16.0, 2: -1.0}), BF16
    )
    second_y = circulant(width_y, {-2: -1.0, -1: 16.0, 1: 16.0, 2: -1.0})
    second_y = jnp.asarray(
        np.concatenate([second_y, np.eye(width_y, dtype=np.float32)], axis=1), BF16
    )
    flat = projectors.reshape(entry_count * proj_count, tile_len)
    moves = other_moves(dom_count)
    places = {u: 0 if u % dom_count == 0 else moves.index(u % dom_count) + 1 for u in range(-2, 3)}
    count = len(moves)
    slots = 3 * band_devices
    applied, forces = pl.pallas_call(
        functools.partial(whole_kernel, dims, dom_count, band_devices, places),
        out_shape=(
            jax.ShapeDtypeStruct(wavefunctions.shape, BF16),
            jax.ShapeDtypeStruct((8, LANES), F32),
        ),
        in_specs=[pl.BlockSpec(memory_space=pl.ANY), vmem(), vmem(), smem(), smem(), vmem(), smem()]
        + [vmem()] * 4,
        out_specs=(pl.BlockSpec(memory_space=pl.ANY), vmem()),
        scratch_shapes=[
            pltpu.VMEM(wavefunctions.shape, BF16),
            pltpu.VMEM(wavefunctions.shape, BF16),
            pltpu.VMEM((2, band_count, 2, width_y, width_z), BF16),
            pltpu.VMEM(((plane_count + 4) * (width_y + 4), band_pad, width_z), BF16),
            pltpu.VMEM((entry_count * proj_count, tile_len), BF16),
            pltpu.VMEM((group, 2 * band_pad, tile_len), BF16),
            pltpu.VMEM((band_pad, lanes), F32),
            pltpu.VMEM((3 * band_pad, lanes), F32),
            pltpu.VMEM((lanes, 3 * LANES), BF16),
            pltpu.VMEM((lanes, 3 * LANES), BF16),
            pltpu.VMEM((row_count, depth * spots), BF16),
            pltpu.VMEM((band_pad, 3 * LANES), BF16),
            pltpu.VMEM((count, band_pad, 3 * LANES), BF16),
            pltpu.VMEM((band_pad, depth * spots, width_z), BF16),
            pltpu.VMEM((row_count, 2 * width_z), BF16),
            pltpu.VMEM((plane_count, width_y, width_z), BF16),
            pltpu.VMEM((band_count, 4, width_y, width_z), F32),
            pltpu.VMEM((row_count, band_pad, width_z), BF16),
            pltpu.VMEM((band_pad, lanes), F32),
            pltpu.VMEM((3, 8, LANES), F32),
            pltpu.VMEM((slots, 8, LANES), F32),
            pltpu.SemaphoreType.DMA,
            pltpu.SemaphoreType.DMA((2,)),
            pltpu.SemaphoreType.DMA((2,)),
            pltpu.SemaphoreType.DMA((count,)),
            pltpu.SemaphoreType.DMA((count,)),
            pltpu.SemaphoreType.DMA((slots,)),
            pltpu.SemaphoreType.DMA((slots,)),
            pltpu.SemaphoreType.DMA((band_count + 2,)),
        ],
        compiler_params=pltpu.CompilerParams(
            vmem_limit_bytes=VMEM_LIMIT, collective_id=0, has_side_effects=True
        ),
        cost_estimate=pl.CostEstimate(
            flops=8 << 30, bytes_accessed=10 << 20, transcendentals=0
        ),
        name="step",
    )(
        wavefunctions, potential, flat, margin_atoms, tile_rows, coupling, band_weights, swap,
        first_z, second_y, second_z,
    )
    return (applied, forces[:3, :ATOM_DEV])


def other_moves(dom_count):
    return sorted({u % dom_count for u in range(-2, 3)} - {0})


def solution(mesh):
    placed = (
        P("band", "dom", None, None),
        P("dom", None, None),
        P("dom", None, None),
        P("dom"),
        P("dom"),
        P(),
        P("band"),
    )
    return jax.shard_map(
        per_device,
        mesh=mesh,
        in_specs=placed,
        out_specs=(P("band", "dom", None, None), P(None, "dom")),
        check_vma=False,
    )
```

```python
import functools

import jax
import jax.numpy as jnp
import numpy as np
from jax import lax
from jax.experimental import pallas as pl
from jax.experimental.pallas import tpu as pltpu
from jax.sharding import PartitionSpec as P

ATOM_DEV = 12
LANES = 128
ROWS = 16
VMEM_LIMIT = 62 * 1024 * 1024
F32 = jnp.float32
BF16 = jnp.bfloat16
HIGHEST = lax.Precision.HIGHEST


def vmem():
    return pl.BlockSpec(memory_space=pltpu.VMEM)


def smem():
    return pl.BlockSpec(memory_space=pltpu.SMEM)


def dot(a, b):
    return jnp.dot(a, b, preferred_element_type=F32)


def dot_nt(a, b, precision=None):
    return lax.dot_general(
        a, b, (((1,), (1,)), ((), ())), precision=precision, preferred_element_type=F32
    )


def circulant(width, taps):
    table = np.zeros((width, width), np.float32)
    for offset, value in taps.items():
        for target in range(width):
            table[(target + offset) % width, target] += value
    return table


def band_swap(band_count, band_pad):
    table = np.zeros((ROWS * band_pad, band_count * ROWS), np.float32)
    for y in range(ROWS):
        for b in range(band_count):
            table[y * band_pad + b, b * ROWS + y] = 1.0
    return table


def pick_groups(whole, count, height, proj_count):
    whole = whole.reshape(count, height, LANES)
    lane = lax.broadcasted_iota(jnp.int32, whole.shape, 2) // proj_count
    item = lax.broadcasted_iota(jnp.int32, whole.shape, 0)
    return jnp.sum(jnp.where(lane == item, whole, 0.0), axis=0)


def turn_pair(swap, left, right):
    return dot(swap, jnp.concatenate([left, right], axis=1)).astype(BF16)


def signal_all(devices):
    barrier = pltpu.get_barrier_semaphore()
    for device in devices:
        pl.semaphore_signal(
            barrier, inc=1, device_id=device, device_id_type=pl.DeviceIdType.MESH
        )


def wait_all(devices):
    pl.semaphore_wait(pltpu.get_barrier_semaphore(), len(devices))


def iota(shape, axis):
    return lax.broadcasted_iota(jnp.int32, shape, axis)


def remote(src, dst, send, recv, device):
    return pltpu.make_async_remote_copy(
        src_ref=src, dst_ref=dst, send_sem=send, recv_sem=recv, device_id=device,
        device_id_type=pl.DeviceIdType.MESH,
    )


def whole_kernel(
    dims, dom_count, band_devices, places, wave_hbm, pot_ref, proj_ref, atoms_ref, rows_ref,
    coupling_ref, weight_ref, swap_ref, first_ref, second_y_ref, second_z_ref,
    out_hbm, force_ref, out_ref, wave_ref, halo_ref, turned_ref, proj_pair_ref, lhs_ref, margin_ref, meas_ref,
    sort_ref, pick_ref, hit_ref, own_ref, table_ref, term_ref, part_ref, scale_ref, edge_ref,
    field_ref, extra_ref, sums_ref, held_ref, load_sem, halo_send, halo_recv, table_send,
    table_recv, force_send, force_recv, out_sem,
):
    band_count, band_pad, plane_count, width_y, entry_count, proj_count, depth = dims
    stride = width_y + 4
    row_count = plane_count * width_y
    group = LANES // proj_count
    lanes = meas_ref.shape[1]
    own = lax.axis_index("dom")
    band = lax.axis_index("band")
    moves = other_moves(dom_count)
    partners = [
        (s, t) for t in range(band_devices) for s in (-1, 0, 1) if (s, t) != (0, 0)
    ]

    def device(s, t):
        return {
            "dom": lax.rem(own + s + dom_count, dom_count),
            "band": lax.rem(band + t, band_devices),
        }

    greeted = sorted({(s % dom_count, t) for s, t in partners} | {(u, 0) for u in moves})
    signal_all([device(s, t) for s, t in greeted])
    load = pltpu.make_async_copy(wave_hbm, wave_ref, load_sem)
    load.start()

    turned_ref[: 2 * stride] = jnp.zeros((2 * stride, band_pad, LANES), BF16)
    turned_ref[(plane_count + 2) * stride :] = jnp.zeros((2 * stride, band_pad, LANES), BF16)
    inner = (plane_count - 4) * width_y
    wait_all(greeted)

    halos = [
        remote(
            wave_hbm.at[:, pl.ds(plane_count - 2, 2)], halo_ref.at[0], halo_send.at[0],
            halo_recv.at[0], device(1, 0),
        ),
        remote(
            wave_hbm.at[:, pl.ds(0, 2)], halo_ref.at[1], halo_send.at[1], halo_recv.at[1],
            device(-1, 0),
        ),
    ]
    for copy in halos:
        copy.start()

    field_ref[2 * width_y : 2 * width_y + inner] = jnp.zeros((inner, band_pad, LANES), BF16)
    spots = lanes // proj_count
    slot_of = iota((entry_count, 3 * LANES), 0)
    atoms = jnp.zeros((entry_count, 3 * LANES), jnp.int32)
    line = jnp.full((8, spots), -4096, jnp.int32)
    for e in range(entry_count):
        atoms = jnp.where(slot_of == e, atoms_ref[e], atoms)
        line = jnp.where(iota((8, spots), 1) == e, rows_ref[e], line)
    weight = jnp.zeros((band_pad, lanes), F32)
    for b in range(band_count):
        weight = jnp.where(iota((band_pad, lanes), 0) == b, -2.0 * weight_ref[b], weight)
    owner = jnp.zeros_like(atoms)
    for k in range(1, dom_count):
        owner = owner + (atoms >= k * ATOM_DEV).astype(jnp.int32)
    within = atoms - owner * ATOM_DEV
    relative = owner - own + 1
    relative = jnp.where(relative < 0, relative + dom_count, relative)
    relative = jnp.where(relative >= dom_count, relative - dom_count, relative)
    target = iota((entry_count, 3 * LANES), 1)
    first_lane = relative * LANES + within * proj_count
    shift = target - first_lane
    near = ((shift >= 0) & (shift < proj_count)).astype(F32).astype(BF16)
    chosen = (target == relative * LANES + within).astype(F32).astype(BF16)
    entry_of = (iota((lanes, entry_count), 0) // proj_count == iota((lanes, entry_count), 1))
    entry_of = entry_of.astype(F32).astype(BF16)
    square = (lanes, 3 * LANES)
    same = iota(square, 0) % proj_count == iota(square, 1) % proj_count
    sort_ref[...] = jnp.where(same, dot(entry_of, near), 0.0).astype(BF16)
    pick_ref[...] = dot(entry_of, chosen).astype(BF16)
    column = iota((spots, depth * spots), 1)
    entry = (column // LANES) * group + column % group
    entry_at = (entry == iota((spots, depth * spots), 0)).astype(F32)
    goal = jnp.dot(
        line.astype(F32), entry_at, precision=HIGHEST, preferred_element_type=F32
    )[:1]
    goal = goal + ((iota(goal.shape, 1) % LANES) // group).astype(F32)
    for x in range(plane_count):
        grid_row = (iota((width_y, depth * spots), 0) + x * width_y).astype(F32)
        hit_ref[x * width_y : (x + 1) * width_y] = (grid_row == goal).astype(F32).astype(BF16)
    scale_ref[...] = (pot_ref[...] * -24.0).astype(BF16)
    square = (LANES, LANES)
    unit = (iota(square, 0) == iota(square, 1)).astype(F32).astype(BF16)
    proj_pair_ref[...] = jnp.zeros_like(proj_pair_ref)
    for j in range(depth):
        turned = dot_nt(unit, proj_ref[:, j * LANES : (j + 1) * LANES]).astype(BF16)
        along_z = (dot(first_ref[...], turned) * (1.0 / 12.0)).astype(BF16)
        for index, start in enumerate(range(0, entry_count, group)):
            first = start * proj_count
            width = min(group, entry_count - start) * proj_count
            rows = slice(j * LANES, (j + 1) * LANES)
            proj_pair_ref[index, rows, :width] = turned[:, first : first + width]
            proj_pair_ref[index, rows, LANES : LANES + width] = along_z[:, first : first + width]
    meas_ref[...] = jnp.zeros_like(meas_ref)
    margin_ref[...] = jnp.zeros_like(margin_ref)
    extra_ref[...] = jnp.zeros_like(extra_ref)
    load.wait()

    def turn(step, carry):
        rows = pl.ds(pl.multiple_of(step * ROWS, ROWS), ROWS)
        blocks = [
            wave_ref[:, x, rows, :].reshape(band_count * ROWS, LANES) for x in range(plane_count)
        ]
        moved = [
            turn_pair(swap_ref[...], blocks[x], blocks[x + 1]) for x in range(0, plane_count, 2)
        ]
        for x in range(plane_count):
            k = x % 2
            turned_ref[pl.ds((x + 2) * stride + 2 + step * ROWS, ROWS)] = moved[x // 2][
                :, k * LANES : (k + 1) * LANES
            ].reshape(ROWS, band_pad, LANES)
        return carry

    lax.fori_loop(0, width_y // ROWS, turn, 0)
    for x in range(2, plane_count + 2):
        base = x * stride
        turned_ref[base : base + 2] = turned_ref[base + width_y : base + width_y + 2]
        turned_ref[base + width_y + 2 : base + width_y + 4] = turned_ref[base + 2 : base + 4]

    bits = width_y.bit_length() - 1

    def place(row, j):
        at = row + j
        return at + 4 * lax.shift_right_logical(at, bits) + 2 * stride + 2

    def each_group(body, height, results):
        for index, start in enumerate(range(0, entry_count, group)):
            count = min(group, entry_count - start)
            first = start * proj_count

            def step(pair, carry):
                tiles = [body(rows_ref[start + 2 * pair + k]) for k in range(2)]
                for k in range(2):
                    lhs_ref[2 * pair + k, :height] = tiles[k]
                return carry

            lax.fori_loop(0, count // 2, step, 0, unroll=2)
            lhs = lhs_ref[:count, :height].reshape(count * height, depth * LANES)
            width = len(results) * LANES
            whole = dot(lhs, proj_pair_ref[index, :, :width])
            for part, (result_ref, low) in enumerate(results):
                result_ref[low : low + height, first : first + LANES] = pick_groups(
                    whole[:, part * LANES : (part + 1) * LANES], count, height, proj_count
                )

    def fetch(row):
        return jnp.concatenate([turned_ref[place(row, j)] for j in range(depth)], axis=1)

    each_group(fetch, band_pad, [(margin_ref, 0), (meas_ref, 2 * band_pad)])
    own_ref[...] = dot(margin_ref[...].astype(BF16), sort_ref[...]).astype(BF16)
    copies = []
    for slot, u in enumerate(moves):
        copy = remote(
            own_ref, table_ref.at[slot], table_send.at[slot], table_recv.at[slot], device(-u, 0)
        )
        copy.start()
        copies.append(copy)

    def derive(row):
        parts = []
        for step in (stride, 1):
            values = []
            for j in range(depth):
                at = place(row, j)
                far = turned_ref[at - 2 * step].astype(F32) - turned_ref[at + 2 * step].astype(F32)
                side = turned_ref[at + step].astype(F32) - turned_ref[at - step].astype(F32)
                values.append((far * (1.0 / 12.0) + side * (2.0 / 3.0)).astype(BF16))
            parts.append(jnp.concatenate(values, axis=1))
        return jnp.concatenate(parts, axis=0)

    each_group(derive, 2 * band_pad, [(meas_ref, 0)])

    for copy in copies:
        copy.wait_recv()
    tables = [own_ref[...]] + [table_ref[slot] for slot in range(len(moves))]
    totals = []
    for s in (-1, 0, 1):
        total = jnp.zeros((band_pad, LANES), F32)
        for u in (s - 1, s, s + 1):
            block = s - u + 1
            total = total + tables[places[u]][:, block * LANES : (block + 1) * LANES].astype(F32)
        totals.append(total)
    inside = (iota((LANES, proj_count), 0) % proj_count == iota((LANES, proj_count), 1)).astype(F32)
    spread = jnp.dot(inside, coupling_ref[...], precision=HIGHEST, preferred_element_type=F32)
    mix = 0.5 * (dot_nt(spread, inside, HIGHEST) + dot_nt(inside, spread, HIGHEST))
    square = (LANES, LANES)
    mix = jnp.where(
        iota(square, 0) // proj_count == iota(square, 1) // proj_count, mix, 0.0
    )
    scaled = jnp.dot(
        jnp.concatenate(totals, axis=0), mix, precision=HIGHEST, preferred_element_type=F32
    )
    scaled = jnp.concatenate(
        [scaled[s * band_pad : (s + 1) * band_pad] for s in range(3)], axis=1
    )
    high = scaled.astype(BF16)
    low = (scaled - high.astype(F32)).astype(BF16)
    sorted_back = dot_nt(jnp.concatenate([high, low], axis=0), sort_ref[...])
    half = sorted_back[:band_pad]
    weighted = (half + sorted_back[band_pad:]) * weight

    for index, start in enumerate(range(0, entry_count, group)):
        width = min(group, entry_count - start) * proj_count
        first = start * proj_count
        shape = (band_pad, group, width)
        held = jnp.broadcast_to(half[:, first : first + width][:, None], shape)
        held = jnp.where(iota(shape, 2) // proj_count == iota(shape, 1), held, 0.0)
        held = held.reshape(band_pad * group, width).astype(BF16)
        for j in range(depth):
            terms = dot(held, proj_ref[first : first + width, j * LANES : (j + 1) * LANES])
            at = index * LANES + j * group
            term_ref[:, at : at + group, :] = (
                (terms * -24.0).astype(BF16).reshape(band_pad, group, LANES)
            )

    def inner_copy(b):
        planes = pl.ds(2, plane_count - 4)
        return pltpu.make_async_copy(
            out_ref.at[b, planes], out_hbm.at[b, planes], out_sem.at[b]
        )

    def edge_copy(side):
        planes = pl.ds(side * (plane_count - 2), 2)
        return pltpu.make_async_copy(
            out_ref.at[:, planes], out_hbm.at[:, planes], out_sem.at[band_count + side]
        )

    def each_pair(pair, carry):
        terms = jnp.concatenate([term_ref[pair * 2], term_ref[pair * 2 + 1]], axis=1)
        part_ref[...] = dot(hit_ref[...], terms).astype(BF16)
        for start in range(0, plane_count, 2):
            totals = []
            for x in (start, start + 1):
                tops, adds = [], []
                for k in range(2):
                    b = pair * 2 + k

                    def near(offset):
                        return [
                            wave_ref[b, x + o]
                            for o in (offset, -offset)
                            if 0 <= x + o < plane_count
                        ]

                    here = wave_ref[b, x]
                    one, two = near(1), near(2)
                    side = sum(one[1:], one[0]) * jnp.asarray(16.0, BF16)
                    side = side - sum(two[1:], two[0])
                    part = part_ref[x * width_y : (x + 1) * width_y, k * LANES : (k + 1) * LANES]
                    adds.append(side + (scale_ref[x] * here + part))
                    tops.append(here)
                both = jnp.concatenate(
                    [jnp.concatenate(tops, axis=1), jnp.concatenate(adds, axis=1)], axis=0
                )
                lap = dot(second_y_ref[...], both)
                along_z = dot(jnp.concatenate(tops, axis=0), second_z_ref[...])
                for k in range(2):
                    total = lap[:, k * LANES : (k + 1) * LANES]
                    total = total + along_z[k * width_y : (k + 1) * width_y]
                    totals.append((pair * 2 + k, x, total * (-1.0 / 24.0)))
            for b, x, total in totals:
                if x < 2:
                    edge_ref[b, x] = total
                elif x >= plane_count - 2:
                    edge_ref[b, x - plane_count + 4] = total
                else:
                    out_ref[b, x] = total.astype(BF16)
        for k in range(2):
            inner_copy(pair * 2 + k).start()
        return carry

    lax.fori_loop(0, band_count // 2, each_pair, 0)

    last = plane_count - 1
    share = 1.0 / 24.0

    def turn_halo(side):
        def halo_rows(pair, carry):
            moved = []
            for k in range(2):
                rows = pl.ds(pl.multiple_of((pair * 2 + k) * ROWS, ROWS), ROWS)
                first = halo_ref[side, :, 0, rows, :].astype(F32)
                second = halo_ref[side, :, 1, rows, :].astype(F32)
                if side == 0:
                    x, left, right = 0, first - 8.0 * second, second
                else:
                    x, left, right = last - 1, -first, 8.0 * first - second
                moved.append(
                    turn_pair(
                        swap_ref[...],
                        *[
                            (value * (1.0 / 12.0)).astype(BF16).reshape(band_count * ROWS, LANES)
                            for value in (left, right)
                        ],
                    )
                )
            for k in range(2):
                for plane in range(2):
                    at = (x + plane) * width_y + (pair * 2 + k) * ROWS
                    field_ref[pl.ds(at, ROWS)] = moved[k][
                        :, plane * LANES : (plane + 1) * LANES
                    ].reshape(ROWS, band_pad, LANES)
            return carry

        lax.fori_loop(0, width_y // ROWS // 2, halo_rows, 0)

    def edge_side(side):
        def edges(b, carry):
            first = halo_ref[side, b, 0].astype(F32)
            second = halo_ref[side, b, 1].astype(F32)
            if side == 0:
                x, left, right = 0, first - 16.0 * second, second
            else:
                x, left, right = last - 1, first, second - 16.0 * first
            left = (edge_ref[b, 2 * side] + left * share).astype(BF16)
            right = (edge_ref[b, 2 * side + 1] + right * share).astype(BF16)
            out_ref[b, x] = left
            out_ref[b, x + 1] = right
            return carry

        lax.fori_loop(0, band_count, edges, 0)
        edge_copy(side).start()

    even = lax.rem(own, 2) == 0

    def on_sides(even_side, body):
        @pl.when(even)
        def _():
            body(even_side)

        @pl.when(jnp.logical_not(even))
        def _():
            body(1 - even_side)

    def near_halo(side):
        halos[side].wait_recv()
        turn_halo(side)
        edge_side(side)

    def far_halo(side):
        halos[side].wait_recv()
        turn_halo(side)

    on_sides(1, near_halo)
    on_sides(0, far_halo)

    def fetch_halo(row):
        return jnp.concatenate([field_ref[row + j] for j in range(depth)], axis=1)

    each_group(fetch_halo, band_pad, [(extra_ref, 0)])
    sums = []
    for k in range(3):
        held = meas_ref[k * band_pad : (k + 1) * band_pad]
        if k == 0:
            held = held + extra_ref[...]
        sums.append(jnp.sum(weighted * held, axis=0, keepdims=True))
    sums = jnp.concatenate(sums + [jnp.zeros((5, lanes), F32)], axis=0)
    high = sums.astype(BF16)
    rest = sums - high.astype(F32)
    middle = rest.astype(BF16)
    low = (rest - middle.astype(F32)).astype(BF16)
    pieces = jnp.concatenate([high, middle, low, jnp.zeros_like(low)], axis=0)
    spread = dot(pieces, pick_ref[...])
    spread = spread[:8] + spread[8:16] + spread[16:24]
    for s in range(3):
        sums_ref[s] = spread[:, s * LANES : (s + 1) * LANES]
    force_copies = []
    for s, t in partners:
        slot = (s + 1) * band_devices + t
        copy = remote(
            sums_ref.at[s + 1], held_ref.at[slot], force_send.at[slot], force_recv.at[slot],
            device(s, t),
        )
        copy.start()
        force_copies.append((slot, copy))

    on_sides(0, edge_side)
    total = sums_ref[1]
    for slot, copy in force_copies:
        copy.wait_recv()
        total = total + held_ref[slot]
    force_ref[...] = total[:3, :ATOM_DEV]
    for copy in halos + copies + [copy for _, copy in force_copies]:
        copy.wait_send()

    def finish(b, carry):
        inner_copy(b).wait()
        return carry

    lax.fori_loop(0, band_count, finish, 0)
    for side in range(2):
        edge_copy(side).wait()


def per_device(
    wavefunctions, potential, projectors, margin_atoms, tile_rows, coupling, band_weights
):
    band_count, plane_count, width_y, width_z = wavefunctions.shape
    entry_count, proj_count, tile_len = projectors.shape
    depth = tile_len // width_z
    row_count = plane_count * width_y
    band_pad = max(band_count, ROWS)
    dims = (band_count, band_pad, plane_count, width_y, entry_count, proj_count, depth)
    dom_count = lax.axis_size("dom")
    band_devices = lax.axis_size("band")
    group = LANES // proj_count
    lanes = -(-entry_count * proj_count // LANES) * LANES
    spots = lanes // proj_count

    swap = jnp.asarray(band_swap(band_count, band_pad), BF16)
    first_z = jnp.asarray(circulant(width_z, {-2: 1.0, -1: -8.0, 1: 8.0, 2: -1.0}), BF16)
    second_z = jnp.asarray(
        circulant(width_z, {-2: -1.0, -1: 16.0, 0: -90.0, 1: 16.0, 2: -1.0}), BF16
    )
    second_y = circulant(width_y, {-2: -1.0, -1: 16.0, 1: 16.0, 2: -1.0})
    second_y = jnp.asarray(
        np.concatenate([second_y, np.eye(width_y, dtype=np.float32)], axis=1), BF16
    )
    flat = projectors.reshape(entry_count * proj_count, tile_len)
    moves = other_moves(dom_count)
    places = {u: 0 if u % dom_count == 0 else moves.index(u % dom_count) + 1 for u in range(-2, 3)}
    count = len(moves)
    slots = 3 * band_devices
    applied, forces = pl.pallas_call(
        functools.partial(whole_kernel, dims, dom_count, band_devices, places),
        out_shape=(
            jax.ShapeDtypeStruct(wavefunctions.shape, BF16),
            jax.ShapeDtypeStruct((3, ATOM_DEV), F32),
        ),
        in_specs=[pl.BlockSpec(memory_space=pl.ANY), vmem(), vmem(), smem(), smem(), vmem(), smem()]
        + [vmem()] * 4,
        out_specs=(pl.BlockSpec(memory_space=pl.ANY), vmem()),
        scratch_shapes=[
            pltpu.VMEM(wavefunctions.shape, BF16),
            pltpu.VMEM(wavefunctions.shape, BF16),
            pltpu.VMEM((2, band_count, 2, width_y, width_z), BF16),
            pltpu.VMEM(((plane_count + 4) * (width_y + 4), band_pad, width_z), BF16),
            pltpu.VMEM((lanes // LANES, tile_len, 2 * LANES), BF16),
            pltpu.VMEM((group, 2 * band_pad, tile_len), BF16),
            pltpu.VMEM((band_pad, lanes), F32),
            pltpu.VMEM((3 * band_pad, lanes), F32),
            pltpu.VMEM((lanes, 3 * LANES), BF16),
            pltpu.VMEM((lanes, 3 * LANES), BF16),
            pltpu.VMEM((row_count, depth * spots), BF16),
            pltpu.VMEM((band_pad, 3 * LANES), BF16),
            pltpu.VMEM((count, band_pad, 3 * LANES), BF16),
            pltpu.VMEM((band_pad, depth * spots, width_z), BF16),
            pltpu.VMEM((row_count, 2 * width_z), BF16),
            pltpu.VMEM((plane_count, width_y, width_z), BF16),
            pltpu.VMEM((band_count, 4, width_y, width_z), F32),
            pltpu.VMEM((row_count, band_pad, width_z), BF16),
            pltpu.VMEM((band_pad, lanes), F32),
            pltpu.VMEM((3, 8, LANES), F32),
            pltpu.VMEM((slots, 8, LANES), F32),
            pltpu.SemaphoreType.DMA,
            pltpu.SemaphoreType.DMA((2,)),
            pltpu.SemaphoreType.DMA((2,)),
            pltpu.SemaphoreType.DMA((count,)),
            pltpu.SemaphoreType.DMA((count,)),
            pltpu.SemaphoreType.DMA((slots,)),
            pltpu.SemaphoreType.DMA((slots,)),
            pltpu.SemaphoreType.DMA((band_count + 2,)),
        ],
        compiler_params=pltpu.CompilerParams(
            vmem_limit_bytes=VMEM_LIMIT, collective_id=0, has_side_effects=True
        ),
        cost_estimate=pl.CostEstimate(
            flops=8 << 30, bytes_accessed=10 << 20, transcendentals=0
        ),
        name="step",
    )(
        wavefunctions, potential, flat, margin_atoms, tile_rows, coupling, band_weights, swap,
        first_z, second_y, second_z,
    )
    return (applied, forces)


def other_moves(dom_count):
    return sorted({u % dom_count for u in range(-2, 3)} - {0})


def solution(mesh):
    placed = (
        P("band", "dom", None, None),
        P("dom", None, None),
        P("dom", None, None),
        P("dom"),
        P("dom"),
        P(),
        P("band"),
    )
    return jax.shard_map(
        per_device,
        mesh=mesh,
        in_specs=placed,
        out_specs=(P("band", "dom", None, None), P(None, "dom")),
        check_vma=False,
    )
```

```python
import functools

import jax
import jax.numpy as jnp
import numpy as np
from jax import lax
from jax.experimental import pallas as pl
from jax.experimental.pallas import tpu as pltpu
from jax.sharding import PartitionSpec as P

ATOM_DEV = 12
LANES = 128
ROWS = 16
HALO_ROWS = 32
VMEM_LIMIT = 62 * 1024 * 1024
F32 = jnp.float32
BF16 = jnp.bfloat16
HIGHEST = lax.Precision.HIGHEST


def vmem():
    return pl.BlockSpec(memory_space=pltpu.VMEM)


def smem():
    return pl.BlockSpec(memory_space=pltpu.SMEM)


def dot(a, b):
    return jnp.dot(a, b, preferred_element_type=F32)


def dot_nt(a, b, precision=None):
    return lax.dot_general(
        a, b, (((1,), (1,)), ((), ())), precision=precision, preferred_element_type=F32
    )


def circulant(width, taps):
    table = np.zeros((width, width), np.float32)
    for offset, value in taps.items():
        for target in range(width):
            table[(target + offset) % width, target] += value
    return table


def band_swap(band_count, band_pad):
    table = np.zeros((ROWS * band_pad, band_count * ROWS), np.float32)
    for y in range(ROWS):
        for b in range(band_count):
            table[y * band_pad + b, b * ROWS + y] = 1.0
    return table


def pick_groups(whole, count, height, proj_count):
    whole = whole.reshape(count, height, LANES)
    lane = lax.broadcasted_iota(jnp.int32, whole.shape, 2) // proj_count
    item = lax.broadcasted_iota(jnp.int32, whole.shape, 0)
    return jnp.sum(jnp.where(lane == item, whole, 0.0), axis=0)


def turn_pair(swap, left, right):
    return dot(swap, jnp.concatenate([left, right], axis=1)).astype(BF16)


def signal_all(devices):
    barrier = pltpu.get_barrier_semaphore()
    for device in devices:
        pl.semaphore_signal(
            barrier, inc=1, device_id=device, device_id_type=pl.DeviceIdType.MESH
        )


def wait_all(devices):
    pl.semaphore_wait(pltpu.get_barrier_semaphore(), len(devices))


def iota(shape, axis):
    return lax.broadcasted_iota(jnp.int32, shape, axis)


def remote(src, dst, send, recv, device):
    return pltpu.make_async_remote_copy(
        src_ref=src, dst_ref=dst, send_sem=send, recv_sem=recv, device_id=device,
        device_id_type=pl.DeviceIdType.MESH,
    )


def whole_kernel(
    dims, dom_count, band_devices, places, wave_hbm, pot_ref, proj_ref, atoms_ref, rows_ref,
    coupling_ref, weight_ref, swap_ref, first_ref, second_y_ref, second_z_ref,
    out_hbm, force_ref, out_ref, wave_ref, halo_ref, turned_ref, proj_pair_ref, lhs_ref, margin_ref, meas_ref,
    sort_ref, pick_ref, hit_ref, own_ref, table_ref, term_ref, part_ref, scale_ref, edge_ref,
    field_ref, extra_ref, sums_ref, held_ref, load_sem, halo_send, halo_recv, table_send,
    table_recv, force_send, force_recv, out_sem,
):
    band_count, band_pad, plane_count, width_y, entry_count, proj_count, depth = dims
    stride = width_y + 4
    row_count = plane_count * width_y
    group = LANES // proj_count
    lanes = meas_ref.shape[1]
    own = lax.axis_index("dom")
    band = lax.axis_index("band")
    moves = other_moves(dom_count)
    partners = [
        (s, t) for t in range(band_devices) for s in (-1, 0, 1) if (s, t) != (0, 0)
    ]

    def device(s, t):
        return {
            "dom": lax.rem(own + s + dom_count, dom_count),
            "band": lax.rem(band + t, band_devices),
        }

    greeted = sorted({(s % dom_count, t) for s, t in partners} | {(u, 0) for u in moves})
    signal_all([device(s, t) for s, t in greeted])
    load = pltpu.make_async_copy(wave_hbm, wave_ref, load_sem)
    load.start()

    turned_ref[: 2 * stride] = jnp.zeros((2 * stride, band_pad, LANES), BF16)
    turned_ref[(plane_count + 2) * stride :] = jnp.zeros((2 * stride, band_pad, LANES), BF16)
    inner = (plane_count - 4) * width_y
    wait_all(greeted)

    pieces = width_y // HALO_ROWS
    halos = []
    for side in range(2):
        planes = pl.ds((plane_count - 2) * (1 - side), 2)
        for piece in range(pieces):
            rows = pl.ds(piece * HALO_ROWS, HALO_ROWS)
            slot = side * pieces + piece
            halos.append(
                remote(
                    wave_hbm.at[:, planes, rows], halo_ref.at[side, :, :, rows],
                    halo_send.at[slot], halo_recv.at[slot], device(1 - 2 * side, 0),
                )
            )
    even = lax.rem(own, 2) == 0

    def on_sides(even_side, body):
        @pl.when(even)
        def _():
            body(even_side)

        @pl.when(jnp.logical_not(even))
        def _():
            body(1 - even_side)

    def start_halo(side):
        for piece in range(pieces):
            halos[side * pieces + piece].start()

    on_sides(1, start_halo)
    on_sides(0, start_halo)

    field_ref[2 * width_y : 2 * width_y + inner] = jnp.zeros((inner, band_pad, LANES), BF16)
    spots = lanes // proj_count
    slot_of = iota((entry_count, 3 * LANES), 0)
    atoms = jnp.zeros((entry_count, 3 * LANES), jnp.int32)
    line = jnp.full((8, spots), -4096, jnp.int32)
    for e in range(entry_count):
        atoms = jnp.where(slot_of == e, atoms_ref[e], atoms)
        line = jnp.where(iota((8, spots), 1) == e, rows_ref[e], line)
    weight = jnp.zeros((band_pad, lanes), F32)
    for b in range(band_count):
        weight = jnp.where(iota((band_pad, lanes), 0) == b, -2.0 * weight_ref[b], weight)
    owner = jnp.zeros_like(atoms)
    for k in range(1, dom_count):
        owner = owner + (atoms >= k * ATOM_DEV).astype(jnp.int32)
    within = atoms - owner * ATOM_DEV
    relative = owner - own + 1
    relative = jnp.where(relative < 0, relative + dom_count, relative)
    relative = jnp.where(relative >= dom_count, relative - dom_count, relative)
    target = iota((entry_count, 3 * LANES), 1)
    first_lane = relative * LANES + within * proj_count
    shift = target - first_lane
    near = ((shift >= 0) & (shift < proj_count)).astype(F32).astype(BF16)
    chosen = (target == relative * LANES + within).astype(F32).astype(BF16)
    entry_of = (iota((lanes, entry_count), 0) // proj_count == iota((lanes, entry_count), 1))
    entry_of = entry_of.astype(F32).astype(BF16)
    square = (lanes, 3 * LANES)
    same = iota(square, 0) % proj_count == iota(square, 1) % proj_count
    sort_ref[...] = jnp.where(same, dot(entry_of, near), 0.0).astype(BF16)
    pick_ref[...] = dot(entry_of, chosen).astype(BF16)
    column = iota((spots, depth * spots), 1)
    entry = (column // LANES) * group + column % group
    entry_at = (entry == iota((spots, depth * spots), 0)).astype(F32)
    goal = jnp.dot(
        line.astype(F32), entry_at, precision=HIGHEST, preferred_element_type=F32
    )[:1]
    goal = goal + ((iota(goal.shape, 1) % LANES) // group).astype(F32)
    for x in range(plane_count):
        grid_row = (iota((width_y, depth * spots), 0) + x * width_y).astype(F32)
        hit_ref[x * width_y : (x + 1) * width_y] = (grid_row == goal).astype(F32).astype(BF16)
    scale_ref[...] = (pot_ref[...] * -24.0).astype(BF16)
    square = (LANES, LANES)
    unit = (iota(square, 0) == iota(square, 1)).astype(F32).astype(BF16)
    proj_pair_ref[...] = jnp.zeros_like(proj_pair_ref)
    for j in range(depth):
        turned = dot_nt(unit, proj_ref[:, j * LANES : (j + 1) * LANES]).astype(BF16)
        along_z = (dot(first_ref[...], turned) * (1.0 / 12.0)).astype(BF16)
        for index, start in enumerate(range(0, entry_count, group)):
            first = start * proj_count
            width = min(group, entry_count - start) * proj_count
            rows = slice(j * LANES, (j + 1) * LANES)
            proj_pair_ref[index, rows, :width] = turned[:, first : first + width]
            proj_pair_ref[index, rows, LANES : LANES + width] = along_z[:, first : first + width]
    meas_ref[...] = jnp.zeros_like(meas_ref)
    margin_ref[...] = jnp.zeros_like(margin_ref)
    extra_ref[...] = jnp.zeros_like(extra_ref)
    load.wait()

    def turn(step, carry):
        rows = pl.ds(pl.multiple_of(step * ROWS, ROWS), ROWS)
        blocks = [
            wave_ref[:, x, rows, :].reshape(band_count * ROWS, LANES) for x in range(plane_count)
        ]
        moved = [
            turn_pair(swap_ref[...], blocks[x], blocks[x + 1]) for x in range(0, plane_count, 2)
        ]
        for x in range(plane_count):
            k = x % 2
            turned_ref[pl.ds((x + 2) * stride + 2 + step * ROWS, ROWS)] = moved[x // 2][
                :, k * LANES : (k + 1) * LANES
            ].reshape(ROWS, band_pad, LANES)
        return carry

    lax.fori_loop(0, width_y // ROWS, turn, 0)
    for x in range(2, plane_count + 2):
        base = x * stride
        turned_ref[base : base + 2] = turned_ref[base + width_y : base + width_y + 2]
        turned_ref[base + width_y + 2 : base + width_y + 4] = turned_ref[base + 2 : base + 4]

    bits = width_y.bit_length() - 1

    def place(row, j):
        at = row + j
        return at + 4 * lax.shift_right_logical(at, bits) + 2 * stride + 2

    def each_group(body, height, results):
        for index, start in enumerate(range(0, entry_count, group)):
            count = min(group, entry_count - start)
            first = start * proj_count

            def step(pair, carry):
                tiles = [body(rows_ref[start + 2 * pair + k]) for k in range(2)]
                for k in range(2):
                    lhs_ref[2 * pair + k, :height] = tiles[k]
                return carry

            lax.fori_loop(0, count // 2, step, 0, unroll=2)
            lhs = lhs_ref[:count, :height].reshape(count * height, depth * LANES)
            width = len(results) * LANES
            whole = dot(lhs, proj_pair_ref[index, :, :width])
            for part, (result_ref, low) in enumerate(results):
                result_ref[low : low + height, first : first + LANES] = pick_groups(
                    whole[:, part * LANES : (part + 1) * LANES], count, height, proj_count
                )

    def fetch(row):
        return jnp.concatenate([turned_ref[place(row, j)] for j in range(depth)], axis=1)

    each_group(fetch, band_pad, [(margin_ref, 0), (meas_ref, 2 * band_pad)])
    own_ref[...] = dot(margin_ref[...].astype(BF16), sort_ref[...]).astype(BF16)
    copies = []
    for slot, u in enumerate(moves):
        copy = remote(
            own_ref, table_ref.at[slot], table_send.at[slot], table_recv.at[slot], device(-u, 0)
        )
        copy.start()
        copies.append(copy)

    def derive(row):
        parts = []
        for step in (stride, 1):
            values = []
            for j in range(depth):
                at = place(row, j)
                far = turned_ref[at - 2 * step].astype(F32) - turned_ref[at + 2 * step].astype(F32)
                side = turned_ref[at + step].astype(F32) - turned_ref[at - step].astype(F32)
                values.append((far * (1.0 / 12.0) + side * (2.0 / 3.0)).astype(BF16))
            parts.append(jnp.concatenate(values, axis=1))
        return jnp.concatenate(parts, axis=0)

    each_group(derive, 2 * band_pad, [(meas_ref, 0)])

    for copy in copies:
        copy.wait_recv()
    tables = [own_ref[...]] + [table_ref[slot] for slot in range(len(moves))]
    totals = []
    for s in (-1, 0, 1):
        total = jnp.zeros((band_pad, LANES), F32)
        for u in (s - 1, s, s + 1):
            block = s - u + 1
            total = total + tables[places[u]][:, block * LANES : (block + 1) * LANES].astype(F32)
        totals.append(total)
    inside = (iota((LANES, proj_count), 0) % proj_count == iota((LANES, proj_count), 1)).astype(F32)
    spread = jnp.dot(inside, coupling_ref[...], precision=HIGHEST, preferred_element_type=F32)
    mix = 0.5 * (dot_nt(spread, inside, HIGHEST) + dot_nt(inside, spread, HIGHEST))
    square = (LANES, LANES)
    mix = jnp.where(
        iota(square, 0) // proj_count == iota(square, 1) // proj_count, mix, 0.0
    )
    scaled = jnp.dot(
        jnp.concatenate(totals, axis=0), mix, precision=HIGHEST, preferred_element_type=F32
    )
    scaled = jnp.concatenate(
        [scaled[s * band_pad : (s + 1) * band_pad] for s in range(3)], axis=1
    )
    high = scaled.astype(BF16)
    low = (scaled - high.astype(F32)).astype(BF16)
    sorted_back = dot_nt(jnp.concatenate([high, low], axis=0), sort_ref[...])
    half = sorted_back[:band_pad]
    weighted = (half + sorted_back[band_pad:]) * weight

    for index, start in enumerate(range(0, entry_count, group)):
        width = min(group, entry_count - start) * proj_count
        first = start * proj_count
        shape = (band_pad, group, width)
        held = jnp.broadcast_to(half[:, first : first + width][:, None], shape)
        held = jnp.where(iota(shape, 2) // proj_count == iota(shape, 1), held, 0.0)
        held = held.reshape(band_pad * group, width).astype(BF16)
        for j in range(depth):
            terms = dot(held, proj_ref[first : first + width, j * LANES : (j + 1) * LANES])
            at = index * LANES + j * group
            term_ref[:, at : at + group, :] = (
                (terms * -24.0).astype(BF16).reshape(band_pad, group, LANES)
            )

    def inner_copy(b):
        planes = pl.ds(2, plane_count - 4)
        return pltpu.make_async_copy(
            out_ref.at[b, planes], out_hbm.at[b, planes], out_sem.at[b]
        )

    def edge_copy(side):
        planes = pl.ds(side * (plane_count - 2), 2)
        return pltpu.make_async_copy(
            out_ref.at[:, planes], out_hbm.at[:, planes], out_sem.at[band_count + side]
        )

    def each_pair(pair, carry):
        terms = jnp.concatenate([term_ref[pair * 2], term_ref[pair * 2 + 1]], axis=1)
        part_ref[...] = dot(hit_ref[...], terms).astype(BF16)
        for start in range(0, plane_count, 2):
            totals = []
            for x in (start, start + 1):
                tops, adds = [], []
                for k in range(2):
                    b = pair * 2 + k

                    def near(offset):
                        return [
                            wave_ref[b, x + o]
                            for o in (offset, -offset)
                            if 0 <= x + o < plane_count
                        ]

                    here = wave_ref[b, x]
                    one, two = near(1), near(2)
                    side = sum(one[1:], one[0]) * jnp.asarray(16.0, BF16)
                    side = side - sum(two[1:], two[0])
                    part = part_ref[x * width_y : (x + 1) * width_y, k * LANES : (k + 1) * LANES]
                    adds.append(side + (scale_ref[x] * here + part))
                    tops.append(here)
                both = jnp.concatenate(
                    [jnp.concatenate(tops, axis=1), jnp.concatenate(adds, axis=1)], axis=0
                )
                lap = dot(second_y_ref[...], both)
                along_z = dot(jnp.concatenate(tops, axis=0), second_z_ref[...])
                for k in range(2):
                    total = lap[:, k * LANES : (k + 1) * LANES]
                    total = total + along_z[k * width_y : (k + 1) * width_y]
                    totals.append((pair * 2 + k, x, total * (-1.0 / 24.0)))
            for b, x, total in totals:
                if x < 2:
                    edge_ref[b, x] = total
                elif x >= plane_count - 2:
                    edge_ref[b, x - plane_count + 4] = total
                else:
                    out_ref[b, x] = total.astype(BF16)
        for k in range(2):
            inner_copy(pair * 2 + k).start()
        return carry

    lax.fori_loop(0, band_count // 2, each_pair, 0)

    last = plane_count - 1
    share = 1.0 / 24.0

    def turn_halo(side):
        def halo_rows(pair):
            moved = []
            for k in range(2):
                rows = pl.ds(pl.multiple_of((pair * 2 + k) * ROWS, ROWS), ROWS)
                first = halo_ref[side, :, 0, rows, :].astype(F32)
                second = halo_ref[side, :, 1, rows, :].astype(F32)
                if side == 0:
                    x, left, right = 0, first - 8.0 * second, second
                else:
                    x, left, right = last - 1, -first, 8.0 * first - second
                moved.append(
                    turn_pair(
                        swap_ref[...],
                        *[
                            (value * (1.0 / 12.0)).astype(BF16).reshape(band_count * ROWS, LANES)
                            for value in (left, right)
                        ],
                    )
                )
            for k in range(2):
                for plane in range(2):
                    at = (x + plane) * width_y + (pair * 2 + k) * ROWS
                    field_ref[pl.ds(at, ROWS)] = moved[k][
                        :, plane * LANES : (plane + 1) * LANES
                    ].reshape(ROWS, band_pad, LANES)

        for piece in range(pieces):
            halos[side * pieces + piece].wait_recv()
            halo_rows(piece)

    def edge_side(side):
        def edges(b, carry):
            first = halo_ref[side, b, 0].astype(F32)
            second = halo_ref[side, b, 1].astype(F32)
            if side == 0:
                x, left, right = 0, first - 16.0 * second, second
            else:
                x, left, right = last - 1, first, second - 16.0 * first
            left = (edge_ref[b, 2 * side] + left * share).astype(BF16)
            right = (edge_ref[b, 2 * side + 1] + right * share).astype(BF16)
            out_ref[b, x] = left
            out_ref[b, x + 1] = right
            return carry

        lax.fori_loop(0, band_count, edges, 0)
        edge_copy(side).start()

    def near_halo(side):
        turn_halo(side)
        edge_side(side)

    on_sides(1, near_halo)
    on_sides(0, turn_halo)

    def fetch_halo(row):
        return jnp.concatenate([field_ref[row + j] for j in range(depth)], axis=1)

    each_group(fetch_halo, band_pad, [(extra_ref, 0)])
    sums = []
    for k in range(3):
        held = meas_ref[k * band_pad : (k + 1) * band_pad]
        if k == 0:
            held = held + extra_ref[...]
        sums.append(jnp.sum(weighted * held, axis=0, keepdims=True))
    sums = jnp.concatenate(sums + [jnp.zeros((5, lanes), F32)], axis=0)
    high = sums.astype(BF16)
    rest = sums - high.astype(F32)
    middle = rest.astype(BF16)
    low = (rest - middle.astype(F32)).astype(BF16)
    pieces = jnp.concatenate([high, middle, low, jnp.zeros_like(low)], axis=0)
    spread = dot(pieces, pick_ref[...])
    spread = spread[:8] + spread[8:16] + spread[16:24]
    for s in range(3):
        sums_ref[s] = spread[:, s * LANES : (s + 1) * LANES]
    force_copies = []
    for s, t in partners:
        slot = (s + 1) * band_devices + t
        copy = remote(
            sums_ref.at[s + 1], held_ref.at[slot], force_send.at[slot], force_recv.at[slot],
            device(s, t),
        )
        copy.start()
        force_copies.append((slot, copy))

    on_sides(0, edge_side)
    total = sums_ref[1]
    for slot, copy in force_copies:
        copy.wait_recv()
        total = total + held_ref[slot]
    force_ref[...] = total[:3, :ATOM_DEV]
    for copy in halos + copies + [copy for _, copy in force_copies]:
        copy.wait_send()

    def finish(b, carry):
        inner_copy(b).wait()
        return carry

    lax.fori_loop(0, band_count, finish, 0)
    for side in range(2):
        edge_copy(side).wait()


def per_device(
    wavefunctions, potential, projectors, margin_atoms, tile_rows, coupling, band_weights
):
    band_count, plane_count, width_y, width_z = wavefunctions.shape
    entry_count, proj_count, tile_len = projectors.shape
    depth = tile_len // width_z
    row_count = plane_count * width_y
    band_pad = max(band_count, ROWS)
    dims = (band_count, band_pad, plane_count, width_y, entry_count, proj_count, depth)
    dom_count = lax.axis_size("dom")
    band_devices = lax.axis_size("band")
    group = LANES // proj_count
    lanes = -(-entry_count * proj_count // LANES) * LANES
    spots = lanes // proj_count

    swap = jnp.asarray(band_swap(band_count, band_pad), BF16)
    first_z = jnp.asarray(circulant(width_z, {-2: 1.0, -1: -8.0, 1: 8.0, 2: -1.0}), BF16)
    second_z = jnp.asarray(
        circulant(width_z, {-2: -1.0, -1: 16.0, 0: -90.0, 1: 16.0, 2: -1.0}), BF16
    )
    second_y = circulant(width_y, {-2: -1.0, -1: 16.0, 1: 16.0, 2: -1.0})
    second_y = jnp.asarray(
        np.concatenate([second_y, np.eye(width_y, dtype=np.float32)], axis=1), BF16
    )
    flat = projectors.reshape(entry_count * proj_count, tile_len)
    moves = other_moves(dom_count)
    places = {u: 0 if u % dom_count == 0 else moves.index(u % dom_count) + 1 for u in range(-2, 3)}
    count = len(moves)
    slots = 3 * band_devices
    applied, forces = pl.pallas_call(
        functools.partial(whole_kernel, dims, dom_count, band_devices, places),
        out_shape=(
            jax.ShapeDtypeStruct(wavefunctions.shape, BF16),
            jax.ShapeDtypeStruct((3, ATOM_DEV), F32),
        ),
        in_specs=[pl.BlockSpec(memory_space=pl.ANY), vmem(), vmem(), smem(), smem(), vmem(), smem()]
        + [vmem()] * 4,
        out_specs=(pl.BlockSpec(memory_space=pl.ANY), vmem()),
        scratch_shapes=[
            pltpu.VMEM(wavefunctions.shape, BF16),
            pltpu.VMEM(wavefunctions.shape, BF16),
            pltpu.VMEM((2, band_count, 2, width_y, width_z), BF16),
            pltpu.VMEM(((plane_count + 4) * (width_y + 4), band_pad, width_z), BF16),
            pltpu.VMEM((lanes // LANES, tile_len, 2 * LANES), BF16),
            pltpu.VMEM((group, 2 * band_pad, tile_len), BF16),
            pltpu.VMEM((band_pad, lanes), F32),
            pltpu.VMEM((3 * band_pad, lanes), F32),
            pltpu.VMEM((lanes, 3 * LANES), BF16),
            pltpu.VMEM((lanes, 3 * LANES), BF16),
            pltpu.VMEM((row_count, depth * spots), BF16),
            pltpu.VMEM((band_pad, 3 * LANES), BF16),
            pltpu.VMEM((count, band_pad, 3 * LANES), BF16),
            pltpu.VMEM((band_pad, depth * spots, width_z), BF16),
            pltpu.VMEM((row_count, 2 * width_z), BF16),
            pltpu.VMEM((plane_count, width_y, width_z), BF16),
            pltpu.VMEM((band_count, 4, width_y, width_z), F32),
            pltpu.VMEM((row_count, band_pad, width_z), BF16),
            pltpu.VMEM((band_pad, lanes), F32),
            pltpu.VMEM((3, 8, LANES), F32),
            pltpu.VMEM((slots, 8, LANES), F32),
            pltpu.SemaphoreType.DMA,
            pltpu.SemaphoreType.DMA((2 * width_y // HALO_ROWS,)),
            pltpu.SemaphoreType.DMA((2 * width_y // HALO_ROWS,)),
            pltpu.SemaphoreType.DMA((count,)),
            pltpu.SemaphoreType.DMA((count,)),
            pltpu.SemaphoreType.DMA((slots,)),
            pltpu.SemaphoreType.DMA((slots,)),
            pltpu.SemaphoreType.DMA((band_count + 2,)),
        ],
        compiler_params=pltpu.CompilerParams(
            vmem_limit_bytes=VMEM_LIMIT, collective_id=0, has_side_effects=True
        ),
        cost_estimate=pl.CostEstimate(
            flops=8 << 30, bytes_accessed=10 << 20, transcendentals=0
        ),
        name="step",
    )(
        wavefunctions, potential, flat, margin_atoms, tile_rows, coupling, band_weights, swap,
        first_z, second_y, second_z,
    )
    return (applied, forces)


def other_moves(dom_count):
    return sorted({u % dom_count for u in range(-2, 3)} - {0})


def solution(mesh):
    placed = (
        P("band", "dom", None, None),
        P("dom", None, None),
        P("dom", None, None),
        P("dom"),
        P("dom"),
        P(),
        P("band"),
    )
    return jax.shard_map(
        per_device,
        mesh=mesh,
        in_specs=placed,
        out_specs=(P("band", "dom", None, None), P(None, "dom")),
        check_vma=False,
    )
```
